512 devices in a mesh: replica: 64 (over x, y, core), tensor: 8 (over z).
Axes of the slice: x: 4, y: 8, z: 8, core: 2. Of those that a mesh axis runs over, the one named last changes fastest.
Arguments:
- tokens: bfloat16 [32768, 1024], P('replica'), may hold values from -6 to 6
- w_in: bfloat16 [1024, 8, 512], P(None, 'tensor'), may hold values from -0.1875 to 0.1875
- w_out: bfloat16 [8, 128, 1024], P('tensor'), may hold values from -0.1875 to 0.1875
- cache_keys: bfloat16 [64, 1024, 8, 128], P('replica', None, 'tensor'), may hold values from -6 to 6
- cache_values: bfloat16 [64, 1024, 8, 128], P('replica', None, 'tensor'), may hold values from -6 to 6
- session_slot: int32 [64], replicated, may hold values from 0 to 63, as said below
- request_session: int32 [4096], P('replica'), may hold values from 0 to 63, as said below
- cand_count: int32 [4096], P('replica'), may hold values from 1 to 8
- hist_len: int32 [64], replicated, may hold values from 256 to 1024
Outputs:
- mixed: bfloat16 [32768, 1024], P(('replica', 'tensor'))
The draws below stay inside these ranges and needn't reach their ends.
Inputs may be any that keep to these rules, and one draw needn't show every extreme that they name: `session_slot`: a permutation of the cache rows; cache row p lies on replica index p. `request_session`: the 64 requests of one replica index name sessions on at most 2 requests per owning replica index; some owning replica index holds the sessions of exactly 2 requests of every replica index.
All inputs are finite; a program needn't handle non-finite values.
Results may differ from the reference program's by a relative error of at most 0.01.
Values may be sent and summed in bfloat16 or wider, within the bound.
No kernel may reach another device: no remote copies, remote signals or barrier semaphores. Data moves between devices by JAX's collectives and lax.ppermute only.
A program may use at most 64 MiB of HBM per device.

```python
import jax
import jax.numpy as jnp
from jax import lax

D = 1024
H = 8
DH = 128
CAND = 8
HIST = 1024
REQ_DEV = 64
SESS_DEV = 1
REQUESTS = 4096
TOKENS = 32768
SESSIONS = 64
MOST = 2
N_REPLICA = 64


def session_plan(key):
    slot_of = jax.random.permutation(jax.random.fold_in(key, 11), SESSIONS).astype(jnp.int32)
    session_at = jnp.argsort(slot_of, stable=True).astype(jnp.int32)
    hot_owner = jax.random.randint(jax.random.fold_in(key, 12), (), 0, N_REPLICA)

    def device_targets(device_key):
        others = jax.random.permutation(jax.random.fold_in(device_key, 1), N_REPLICA - 1).astype(jnp.int32)
        others = others + (others >= hot_owner).astype(jnp.int32)
        owners = jnp.concatenate([jnp.reshape(hot_owner, (1,)).astype(jnp.int32), others])
        listing = jnp.repeat(owners, MOST)
        tail = jax.random.permutation(jax.random.fold_in(device_key, 2), N_REPLICA * MOST - MOST) + MOST
        chosen = jnp.concatenate([jnp.arange(MOST), tail])[:REQ_DEV]
        targets = jax.random.permutation(jax.random.fold_in(device_key, 3), listing[chosen])
        within = jax.random.randint(jax.random.fold_in(device_key, 4), (REQ_DEV,), 0, SESS_DEV)
        return session_at[targets * SESS_DEV + within]
    device_keys = jax.random.split(jax.random.fold_in(key, 13), N_REPLICA)
    sessions = jax.vmap(device_targets)(device_keys).reshape(-1).astype(jnp.int32)
    return (slot_of, sessions)


def draw_session_slot(key, part):
    shared = session_plan(key)
    return shared[0]


def draw_request_session(key, part):
    shared = session_plan(key)
    return shared[1]


def draw_cand_count(key, part):
    key = jax.random.fold_in(key, 3)
    counts = jax.random.randint(key, (REQUESTS,), 1, CAND + 1).astype(jnp.int32)
    return counts.at[0].set(CAND)


def draw_hist_len(key, part):
    key = jax.random.fold_in(key, 4)
    lengths = jax.random.randint(key, (SESSIONS,), HIST // 4, HIST + 1).astype(jnp.int32)
    return lengths.at[0].set(HIST)


def levels(rng, extent, cuts, least, largest):
    loudness = 1.0
    for axis_at, shards_of in cuts:
        heights = jax.random.uniform(jax.random.fold_in(jax.random.fold_in(rng, 6), axis_at), (shards_of,), jnp.float32, least / len(cuts), largest / len(cuts))
        loudness = loudness * jnp.repeat(jnp.exp(heights), extent[axis_at] // shards_of).reshape((-1,) + (1,) * (len(extent) - 1 - axis_at))
    return loudness


def scatter_about(key, extent, width, reach, cuts=(), kind=jnp.bfloat16):
    values = jax.random.normal(key, extent, jnp.float32) * width
    if len(cuts) > 0:
        values = levels(key, extent, cuts, -0.22, 0.18) * values
    return jnp.clip(values, min=-reach, max=reach).astype(kind)


def setup_inputs(seed: int = 0) -> dict:
    keys = jax.random.split(jax.random.key(seed), 10)
    tokens = scatter_about(keys[0], (TOKENS, D), 1.0, 6.0, ((0, 64),))
    w_in = scatter_about(keys[1], (D, H, 4 * DH), D ** -0.5, 0.1875, ((1, 8),))
    w_out = scatter_about(keys[2], (H, DH, D), (H * DH) ** -0.5, 0.1875, ((0, 8),))
    cache_keys = scatter_about(keys[3], (SESSIONS, HIST, H, DH), 1.0, 6.0, ((0, 64), (2, 8)))
    cache_values = scatter_about(keys[4], (SESSIONS, HIST, H, DH), 1.0, 6.0, ((0, 64), (2, 8)))
    session_slot = draw_session_slot(jax.random.fold_in(keys[9], 71), 0)
    request_session = draw_request_session(jax.random.fold_in(keys[9], 71), 0)
    cand_count = draw_cand_count(jax.random.fold_in(keys[9], 71), 0)
    hist_len = draw_hist_len(jax.random.fold_in(keys[9], 71), 0)
    return dict(tokens=tokens, w_in=w_in, w_out=w_out, cache_keys=cache_keys, cache_values=cache_values, session_slot=session_slot, request_session=request_session, cand_count=cand_count, hist_len=hist_len)


epsilon = 1e-05

def layer_norm(values):
    average = lax.optimization_barrier(jnp.mean(values, -1, keepdims=True))
    centred = values - average
    return centred * lax.rsqrt(lax.optimization_barrier(jnp.mean(centred * centred, -1, keepdims=True)) + epsilon)

def reference(tokens, w_in, w_out, cache_keys, cache_values, session_slot, request_session, cand_count, hist_len):
    inputs = tokens.astype(jnp.float32)
    normed = layer_norm(inputs).astype(jnp.bfloat16)
    projected = jax.nn.silu(jnp.dot(normed, w_in.reshape(D, H * 4 * DH), preferred_element_type=jnp.float32)).astype(jnp.bfloat16)
    projected = projected.reshape(REQUESTS, CAND, H, 4 * DH)
    gate_units = projected[..., :DH]
    cand_values = projected[..., DH:2 * DH]
    queries = projected[..., 2 * DH:3 * DH]
    cand_keys = projected[..., 3 * DH:]
    cache_row = jnp.take(session_slot, request_session).astype(jnp.int32)
    lengths = jnp.take(hist_len, request_session).astype(jnp.int32)
    score_scale = DH ** (-0.5)

    def attend_one(packed):
        query_block, row_index, length = packed
        key_rows = lax.dynamic_index_in_dim(cache_keys, row_index, 0, keepdims=False).astype(jnp.float32)
        value_rows = lax.dynamic_index_in_dim(cache_values, row_index, 0, keepdims=False).astype(jnp.float32)
        scores = jnp.einsum('chd,jhd->hcj', query_block.astype(jnp.float32), key_rows) * score_scale
        visible = (jnp.arange(HIST, dtype=jnp.int32) < length).astype(jnp.float32)
        weights = (jax.nn.silu(scores) * visible).astype(jnp.bfloat16)
        summed = jnp.einsum('hcj,jhd->chd', weights.astype(jnp.float32), value_rows)
        return (summed / (length + 1).astype(jnp.float32)).astype(jnp.bfloat16)
    hist_part = lax.map(attend_one, (queries, cache_row, lengths))
    own_scores = lax.optimization_barrier(jnp.sum(queries.astype(jnp.float32) * cand_keys.astype(jnp.float32), -1, keepdims=True)) * score_scale
    own_term = jax.nn.silu(own_scores) * cand_values.astype(jnp.float32) / (lengths + 1).astype(jnp.float32)[:, None, None, None]
    alive_rows = (jnp.arange(CAND, dtype=jnp.int32)[None, :] < cand_count[:, None]).astype(jnp.float32)
    attended = (hist_part.astype(jnp.float32) + own_term) * alive_rows[:, :, None, None]
    gated = (layer_norm(attended) * gate_units.astype(jnp.float32)).astype(jnp.bfloat16)
    summed_out = jnp.dot(gated.reshape(TOKENS, H * DH), w_out.reshape(H * DH, D), preferred_element_type=jnp.float32)
    return (inputs + summed_out).astype(jnp.bfloat16)
```

```python
import functools

import jax
import jax.numpy as jnp
from jax import lax
from jax.experimental import pallas as pl
from jax.experimental.pallas import tpu as pltpu
from jax.sharding import PartitionSpec as P

epsilon = 1e-05
f32 = jnp.float32
bf16 = jnp.bfloat16


def layer_norm(values):
    average = jnp.mean(values, -1, keepdims=True)
    centred = values - average
    return centred * lax.rsqrt(jnp.mean(centred * centred, -1, keepdims=True) + epsilon)


def silu(values):
    half = values * 0.5
    return half + half * jnp.tanh(half)


def iota(shape, dimension):
    return lax.broadcasted_iota(jnp.int32, shape, dimension)


def to_column(row):
    n = row.shape[1]
    return jnp.sum(jnp.where(iota((n, n), 0) == iota((n, n), 1), row, 0.0), 1, keepdims=True)


def lookup(table_row, index_row):
    sessions, requests = table_row.shape[1], index_row.shape[1]
    named = iota((sessions, requests), 0) == index_row
    return jnp.sum(jnp.where(named, to_column(table_row.astype(f32)), 0.0), 0, keepdims=True)


def first_rows(slot_ref, session_ref, capacity, cands):
    owner = lookup(slot_ref[...], session_ref[...])
    requests = owner.shape[1]
    square = (requests, requests)
    earlier = (to_column(owner) == owner) & (iota(square, 0) < iota(square, 1))
    rank = jnp.sum(jnp.where(earlier, 1.0, 0.0), 0, keepdims=True)
    return (owner * capacity + rank) * cands


def send_kernel(capacity, cands, tokens_ref, w_ref, slot_ref, session_ref, sent_ref):
    rows = tokens_ref.shape[0]
    head_dim = w_ref.shape[1]
    slot_rows = sent_ref.shape[0]
    normed = layer_norm(tokens_ref[...].astype(f32)).astype(bf16)
    queries = silu(jnp.dot(normed, w_ref[...], preferred_element_type=f32)).astype(bf16)
    first = first_rows(slot_ref, session_ref, capacity, cands)
    requests = first.shape[1]
    spread = iota((requests, rows), 1) // cands == iota((requests, rows), 0)
    place = jnp.sum(jnp.where(spread, to_column(first), 0.0), 0, keepdims=True).astype(jnp.int32)
    place = place + iota((1, rows), 1) % cands
    chosen = jnp.where(iota((slot_rows, rows), 0) == place, 1.0, 0.0).astype(bf16)
    sent_ref[...] = jnp.dot(chosen, queries, preferred_element_type=f32).astype(bf16)


def local_kernel(
    capacity, cands, tokens_ref, w_ref, slot_ref, session_ref, count_ref, length_ref, own_ref, gate_ref, back_ref
):
    rows = tokens_ref.shape[0]
    head_dim = own_ref.shape[1]
    slot_rows = back_ref.shape[1]
    normed = layer_norm(tokens_ref[...].astype(f32)).astype(bf16)
    projected = silu(jnp.dot(normed, w_ref[...], preferred_element_type=f32)).astype(bf16).astype(f32)
    gate = projected[:, :head_dim]
    values = projected[:, head_dim : 2 * head_dim]
    queries = projected[:, 2 * head_dim : 3 * head_dim]
    keys = projected[:, 3 * head_dim :]
    first = first_rows(slot_ref, session_ref, capacity, cands)
    lengths = lookup(length_ref[...], session_ref[...])
    requests = first.shape[1]
    spread = iota((rows, requests), 0) // cands == iota((rows, requests), 1)

    def per_row(row):
        return jnp.sum(jnp.where(spread, row, 0.0), 1, keepdims=True)

    within = iota((rows, 1), 0) % cands
    place = per_row(first).astype(jnp.int32) + within
    back_ref[...] = jnp.where(iota((rows, slot_rows), 1) == place, 1.0, 0.0).astype(bf16)
    scores = jnp.sum(queries * keys, -1, keepdims=True) * head_dim ** (-0.5)
    own_ref[...] = silu(scores) * values / (per_row(lengths) + 1.0)
    alive = within.astype(f32) < per_row(count_ref[...].astype(f32))
    gate_ref[...] = jnp.where(alive, gate, 0.0).astype(bf16)


def history_kernel(block, me_ref, query_ref, keys_ref, values_ref, slot_ref, length_ref, out_ref):
    history, head_dim = keys_ref.shape
    mine = slot_ref[...] == me_ref[0]
    length = jnp.sum(jnp.where(mine, length_ref[...].astype(f32), 0.0), 1, keepdims=True)
    seen = iota((history, 1), 0).astype(f32) < length
    values = jnp.where(seen, values_ref[...], jnp.zeros((), bf16))
    keys = keys_ref[...]
    half_scale = 0.5 * head_dim ** (-0.5)
    for start in range(0, query_ref.shape[0], block):
        half = (
            lax.dot_general(
                query_ref[pl.ds(start, block), :], keys, (((1,), (1,)), ((), ())), preferred_element_type=f32
            )
            * half_scale
        )
        weights = (half + half * jnp.tanh(half)).astype(bf16)
        summed = jnp.dot(weights, values, preferred_element_type=f32)
        out_ref[pl.ds(start, block), :] = (summed / (length + 1.0)).astype(bf16)


def gate_kernel(returned_ref, back_ref, own_ref, gate_ref, out_ref):
    part = jnp.dot(back_ref[...], returned_ref[...], preferred_element_type=f32)
    out_ref[...] = (layer_norm(part + own_ref[...]) * gate_ref[...].astype(f32)).astype(bf16)


def output_kernel(group_ref, gated_ref, w_ref, tokens_ref, out_ref):
    total = tokens_ref[...].astype(f32)
    for head in range(gated_ref.shape[0]):
        total = total + jnp.dot(gated_ref[head], w_ref[head], preferred_element_type=f32)
    out_ref[...] = total.astype(bf16)


VMEM = pl.BlockSpec(memory_space=pltpu.VMEM)
SMEM = pl.BlockSpec(memory_space=pltpu.SMEM)
params = pltpu.CompilerParams(vmem_limit_bytes=40 * 1024 * 1024)


def on_device(
    tokens,
    w_in,
    w_out,
    cache_keys,
    cache_values,
    session_slot,
    request_session,
    cand_count,
    hist_len,
):
    replicas = lax.axis_size("replica")
    groups = lax.axis_size("tensor")
    my_index = lax.axis_index("replica").astype(jnp.int32).reshape(1)
    group_index = lax.axis_index("tensor").astype(jnp.int32).reshape(1)
    rows, model_width = tokens.shape
    head_dim = w_in.shape[2] // 4
    requests = request_session.shape[0]
    cands = rows // requests
    history = cache_keys.shape[1]
    capacity = max(2, (2 * requests + replicas - 1) // replicas)
    slot_rows = replicas * capacity * cands
    w_flat = w_in.reshape(model_width, 4 * head_dim)
    slots = session_slot.reshape(1, -1)
    lengths = hist_len.reshape(1, -1)
    named = request_session.reshape(1, -1)
    counts = cand_count.reshape(1, -1)
    w_whole = lax.all_gather(w_out, "tensor", axis=0, tiled=True)

    sent = pl.pallas_call(
        functools.partial(send_kernel, capacity, cands),
        grid=(1,),
        in_specs=[
            pl.BlockSpec((rows, model_width), lambda i: (0, 0)),
            pl.BlockSpec((model_width, head_dim), lambda i: (0, 2)),
            pl.BlockSpec((1, slots.shape[1]), lambda i: (0, 0)),
            pl.BlockSpec((1, requests), lambda i: (0, 0)),
        ],
        out_specs=pl.BlockSpec((slot_rows, head_dim), lambda i: (0, 0)),
        out_shape=jax.ShapeDtypeStruct((slot_rows, head_dim), bf16),
        compiler_params=params,
        name="send",
    )(tokens, w_flat, slots, named)
    got = lax.all_to_all(
        sent.reshape(replicas, capacity * cands, head_dim), "replica", split_axis=0, concat_axis=0, tiled=True
    )
    own, gate, back = pl.pallas_call(
        functools.partial(local_kernel, capacity, cands),
        in_specs=[VMEM] * 6,
        out_specs=[VMEM] * 3,
        out_shape=[
            jax.ShapeDtypeStruct((rows, head_dim), f32),
            jax.ShapeDtypeStruct((rows, head_dim), bf16),
            jax.ShapeDtypeStruct((rows, slot_rows), bf16),
        ],
        compiler_params=params,
        cost_estimate=pl.CostEstimate(
            flops=2 * rows * model_width * 4 * head_dim, bytes_accessed=4 << 20, transcendentals=rows * 4 * head_dim
        ),
        name="local",
    )(tokens, w_flat, slots, named, counts, lengths)
    answers = pl.pallas_call(
        functools.partial(history_kernel, min(256, slot_rows)),
        in_specs=[SMEM] + [VMEM] * 5,
        out_specs=VMEM,
        out_shape=jax.ShapeDtypeStruct((slot_rows, head_dim), bf16),
        compiler_params=params,
        name="history",
    )(
        my_index,
        got.reshape(slot_rows, head_dim),
        cache_keys.reshape(history, head_dim),
        cache_values.reshape(history, head_dim),
        slots,
        lengths,
    )
    returned = lax.all_to_all(
        answers.reshape(replicas, capacity * cands, head_dim), "replica", split_axis=0, concat_axis=0, tiled=True
    )
    gated = pl.pallas_call(
        gate_kernel,
        in_specs=[VMEM] * 4,
        out_specs=VMEM,
        out_shape=jax.ShapeDtypeStruct((rows, head_dim), bf16),
        compiler_params=params,
        name="gate",
    )(returned.reshape(slot_rows, head_dim), back, own, gate)
    share = rows // groups
    heads = lax.all_to_all(
        gated.reshape(groups, share, head_dim), "tensor", split_axis=0, concat_axis=0, tiled=True
    )
    return pl.pallas_call(
        output_kernel,
        grid_spec=pltpu.PrefetchScalarGridSpec(
            num_scalar_prefetch=1,
            grid=(1,),
            in_specs=[
                pl.BlockSpec((groups, share, head_dim), lambda i, g: (0, 0, 0)),
                pl.BlockSpec((groups, head_dim, model_width), lambda i, g: (0, 0, 0)),
                pl.BlockSpec((share, model_width), lambda i, g: (g[0], 0)),
            ],
            out_specs=pl.BlockSpec((share, model_width), lambda i, g: (0, 0)),
        ),
        out_shape=jax.ShapeDtypeStruct((share, model_width), bf16),
        compiler_params=params,
        name="output",
    )(group_index, heads, w_whole, tokens)


def solution(mesh):
    in_specs = (
        P("replica", None),
        P(None, "tensor", None),
        P("tensor", None, None),
        P("replica", None, "tensor", None),
        P("replica", None, "tensor", None),
        P(),
        P("replica"),
        P("replica"),
        P(),
    )
    out_specs = P(("replica", "tensor"), None)
    return jax.shard_map(
        on_device, mesh=mesh, in_specs=in_specs, out_specs=out_specs, check_vma=False
    )
```

```python
import functools

import jax
import jax.numpy as jnp
from jax import lax
from jax.experimental import pallas as pl
from jax.experimental.pallas import tpu as pltpu
from jax.sharding import PartitionSpec as P

epsilon = 1e-05
f32 = jnp.float32
bf16 = jnp.bfloat16


def layer_norm(values):
    average = jnp.mean(values, -1, keepdims=True)
    centred = values - average
    return centred * lax.rsqrt(jnp.mean(centred * centred, -1, keepdims=True) + epsilon)


def silu(values):
    half = values * 0.5
    return half + half * jnp.tanh(half)


def iota(shape, dimension):
    return lax.broadcasted_iota(jnp.int32, shape, dimension)


def to_column(row):
    n = row.shape[1]
    return jnp.sum(jnp.where(iota((n, n), 0) == iota((n, n), 1), row, 0.0), 1, keepdims=True)


def lookup(table_row, index_row):
    sessions, requests = table_row.shape[1], index_row.shape[1]
    named = iota((sessions, requests), 0) == index_row
    return jnp.sum(jnp.where(named, to_column(table_row.astype(f32)), 0.0), 0, keepdims=True)


def first_rows(slot_ref, session_ref, capacity, cands):
    owner = lookup(slot_ref[...], session_ref[...])
    requests = owner.shape[1]
    square = (requests, requests)
    earlier = (to_column(owner) == owner) & (iota(square, 0) < iota(square, 1))
    rank = jnp.sum(jnp.where(earlier, 1.0, 0.0), 0, keepdims=True)
    return (owner * capacity + rank) * cands


def send_kernel(
    capacity, cands, chunks, tokens_ref, w_ref, slot_ref, session_ref, sent_ref, held, weight, queries, placed, sems, w_sem, out_sems
):
    rows = tokens_ref.shape[0]
    head_dim = weight.shape[1]
    slot_rows = sent_ref.shape[0]
    chunk = rows // chunks
    fetch_w = pltpu.make_async_copy(w_ref.at[:, pl.ds(2 * head_dim, head_dim)], weight, w_sem)
    fetches = [
        pltpu.make_async_copy(
            tokens_ref.at[pl.ds(n * chunk, chunk), :], held.at[pl.ds(n * chunk, chunk), :], sems.at[n]
        )
        for n in range(chunks)
    ]
    fetches[0].start()
    fetch_w.start()
    for fetch in fetches[1:]:
        fetch.start()
    first = first_rows(slot_ref, session_ref, capacity, cands)
    requests = first.shape[1]
    spread = iota((requests, rows), 1) // cands == iota((requests, rows), 0)
    place = jnp.sum(jnp.where(spread, to_column(first), 0.0), 0, keepdims=True).astype(jnp.int32)
    place = place + iota((1, rows), 1) % cands
    for n, fetch in enumerate(fetches):
        part = pl.ds(n * chunk, chunk)
        fetch.wait()
        normed = layer_norm(held[part, :].astype(f32)).astype(bf16)
        if n == 0:
            fetch_w.wait()
        queries[part, :] = silu(jnp.dot(normed, weight[...], preferred_element_type=f32)).astype(bf16)
    block = slot_rows // chunks
    stores = []
    for n in range(chunks):
        part = pl.ds(n * block, block)
        chosen = jnp.where(iota((block, rows), 0) + n * block == place, 1.0, 0.0).astype(bf16)
        placed[part, :] = jnp.dot(chosen, queries[...], preferred_element_type=f32).astype(bf16)
        stores.append(pltpu.make_async_copy(placed.at[part, :], sent_ref.at[part, :], out_sems.at[n]))
        stores[-1].start()
    for store in stores:
        store.wait()


def local_kernel(
    capacity, cands, tokens_ref, w_ref, slot_ref, session_ref, count_ref, length_ref, out_ref, result, sem
):
    rows = tokens_ref.shape[0]
    head_dim = result.shape[1] // 3
    normed = layer_norm(tokens_ref[...].astype(f32)).astype(bf16)
    projected = silu(jnp.dot(normed, w_ref[...], preferred_element_type=f32)).astype(bf16).astype(f32)
    gate = projected[:, :head_dim]
    values = projected[:, head_dim : 2 * head_dim]
    queries = projected[:, 2 * head_dim : 3 * head_dim]
    keys = projected[:, 3 * head_dim :]
    lengths = lookup(length_ref[...], session_ref[...])
    requests = lengths.shape[1]
    spread = iota((rows, requests), 0) // cands == iota((rows, requests), 1)

    def per_row(row):
        return jnp.sum(jnp.where(spread, row, 0.0), 1, keepdims=True)

    within = (iota((rows, 1), 0) % cands).astype(f32)
    scores = jnp.sum(queries * keys, -1, keepdims=True) * head_dim ** (-0.5)
    result[:, :head_dim] = silu(scores) * values / (per_row(lengths) + 1.0)
    alive = within < per_row(count_ref[...].astype(f32))
    result[:, head_dim : 2 * head_dim] = jnp.where(alive, gate, 0.0)
    place = per_row(first_rows(slot_ref, session_ref, capacity, cands)) + within
    result[:, 2 * head_dim :] = jnp.broadcast_to(place, (rows, head_dim))
    store = pltpu.make_async_copy(result, out_ref, sem)
    store.start()
    store.wait()


def history_kernel(
    block, me_ref, slot_ref, length_ref, query_ref, keys_ref, values_ref, out_ref, query, keys, values, result, sems
):
    fetches = [
        pltpu.make_async_copy(source, target, sems.at[n])
        for n, (source, target) in enumerate(((keys_ref, keys), (query_ref, query), (values_ref, values)))
    ]
    for fetch in fetches:
        fetch.start()
    history, head_dim = keys_ref.shape
    length = jnp.zeros((), jnp.int32)
    for session in range(slot_ref.shape[0]):
        length = jnp.where(slot_ref[session] == me_ref[0], length_ref[session], length)
    seen = iota((history, 1), 0) < length
    divisor = (length + 1).astype(f32)
    half_scale = 0.5 * head_dim ** (-0.5)
    fetches[0].wait()
    fetches[1].wait()
    fetches[2].wait()
    seen_values = jnp.where(seen, values[...], jnp.zeros((), bf16))
    stores = []
    for n, start in enumerate(range(0, query_ref.shape[0], block)):
        part = pl.ds(start, block)
        half = (
            lax.dot_general(query[part, :], keys[...], (((1,), (1,)), ((), ())), preferred_element_type=f32)
            * half_scale
        )
        weights = (half + half * jnp.tanh(half)).astype(bf16)
        summed = jnp.dot(weights, seen_values, preferred_element_type=f32)
        result[part, :] = (summed / divisor).astype(bf16)
        stores.append(pltpu.make_async_copy(result.at[part, :], out_ref.at[part, :], sems.at[3 + n]))
        stores[-1].start()
    for store in stores:
        store.wait()


def gate_kernel(returned_ref, mine_ref, out_ref, returned, mine, result, sems):
    fetches = [
        pltpu.make_async_copy(mine_ref, mine, sems.at[0]),
        pltpu.make_async_copy(returned_ref, returned, sems.at[1]),
    ]
    for fetch in fetches:
        fetch.start()
    rows, head_dim = result.shape
    slot_rows = returned.shape[0]
    fetches[0].wait()
    place = mine[:, 2 * head_dim : 2 * head_dim + 1].astype(jnp.int32)
    back = jnp.where(iota((rows, slot_rows), 1) == place, 1.0, 0.0).astype(bf16)
    fetches[1].wait()
    part = jnp.dot(back, returned[...], preferred_element_type=f32)
    result[...] = (layer_norm(part + mine[:, :head_dim]) * mine[:, head_dim : 2 * head_dim]).astype(bf16)
    store = pltpu.make_async_copy(result, out_ref, sems.at[0])
    store.start()
    store.wait()


def output_kernel(group_ref, tokens_ref, gated_ref, *refs):
    groups = gated_ref.shape[0]
    pieces, (out_ref, gated, weight, tokens, result, sems) = refs[:groups], refs[groups:]
    head_dim = gated_ref.shape[2]
    share = out_ref.shape[0]
    me = group_ref[0]
    fetches = [pltpu.make_async_copy(gated_ref, gated, sems.at[groups])]
    for n, piece in enumerate(pieces):
        fetches.append(
            pltpu.make_async_copy(piece, weight.at[pl.ds(n * head_dim, head_dim), :], sems.at[n])
        )
    mine = pl.ds(pl.multiple_of(me * share, share), share)
    fetch_tokens = pltpu.make_async_copy(tokens_ref.at[mine, :], tokens, sems.at[groups + 1])
    for fetch in fetches:
        fetch.start()
    fetch_tokens.start()
    total = jnp.zeros(result.shape, f32)
    fetches[0].wait()
    for n in range(0, groups, 2):
        fetches[1 + n].wait()
        fetches[2 + n].wait()
        pair = jnp.concatenate(
            [gated[lax.rem(me + shift + groups, groups)] for shift in ring_order(groups)[n : n + 2]], axis=1
        )
        total = total + jnp.dot(
            pair, weight[pl.ds(n * head_dim, 2 * head_dim), :], preferred_element_type=f32
        )
    fetch_tokens.wait()
    result[...] = (tokens[...].astype(f32) + total).astype(bf16)
    store = pltpu.make_async_copy(result, out_ref, sems.at[groups])
    store.start()
    store.wait()


def ring_order(groups):
    order = [0]
    for step in range(1, groups // 2 + 1):
        order.append(-step)
        if 2 * step < groups:
            order.append(step)
    return order


ANY = pl.BlockSpec(memory_space=pl.ANY)
HBM = pl.BlockSpec(memory_space=pltpu.HBM)
VMEM = pl.BlockSpec(memory_space=pltpu.VMEM)
SMEM = pl.BlockSpec(memory_space=pltpu.SMEM)
params = pltpu.CompilerParams(vmem_limit_bytes=63 * 1024 * 1024)
tight = pltpu.CompilerParams(vmem_limit_bytes=54528 * 1024)
roomy = pltpu.CompilerParams(vmem_limit_bytes=24 * 1024 * 1024)


def on_device(
    tokens,
    w_in,
    w_out,
    cache_keys,
    cache_values,
    session_slot,
    request_session,
    cand_count,
    hist_len,
):
    replicas = lax.axis_size("replica")
    groups = lax.axis_size("tensor")
    my_index = lax.axis_index("replica").astype(jnp.int32).reshape(1)
    group_index = lax.axis_index("tensor").astype(jnp.int32).reshape(1)
    rows, model_width = tokens.shape
    head_dim = w_in.shape[2] // 4
    requests = request_session.shape[0]
    cands = rows // requests
    history = cache_keys.shape[1]
    capacity = max(2, (2 * requests + replicas - 1) // replicas)
    slot_rows = replicas * capacity * cands
    w_flat = w_in.reshape(model_width, 4 * head_dim)
    slots = session_slot.reshape(1, -1)
    lengths = hist_len.reshape(1, -1)
    named = request_session.reshape(1, -1)
    counts = cand_count.reshape(1, -1)
    chunks = 4

    sent = pl.pallas_call(
        functools.partial(send_kernel, capacity, cands, chunks),
        in_specs=[HBM, HBM, VMEM, VMEM],
        out_specs=HBM,
        out_shape=jax.ShapeDtypeStruct((slot_rows, head_dim), bf16),
        scratch_shapes=[
            pltpu.VMEM((rows, model_width), bf16),
            pltpu.VMEM((model_width, head_dim), bf16),
            pltpu.VMEM((rows, head_dim), bf16),
            pltpu.VMEM((slot_rows, head_dim), bf16),
            pltpu.SemaphoreType.DMA((chunks,)),
            pltpu.SemaphoreType.DMA,
            pltpu.SemaphoreType.DMA((chunks,)),
        ],
        compiler_params=params,
        name="send",
    )(tokens, w_flat, slots, named)
    got = lax.all_to_all(
        sent.reshape(replicas, capacity * cands, head_dim), "replica", split_axis=0, concat_axis=0, tiled=True
    )
    w_own, sent = lax.optimization_barrier((w_out.reshape(head_dim, model_width), sent))

    def shifted(piece, by):
        return lax.ppermute(piece, "tensor", [(z, (z + by) % groups) for z in range(groups)])

    pieces = {0: w_own}
    half = groups // 2
    near = (half + 1) // 2
    for step in range(1, near + 1):
        pieces[-step] = shifted(w_own, step)
        pieces[step] = shifted(w_own, -step)
    block = min(256, slot_rows)
    answers = pl.pallas_call(
        functools.partial(history_kernel, block),
        in_specs=[SMEM, SMEM, SMEM, ANY, HBM, HBM],
        out_specs=HBM,
        out_shape=jax.ShapeDtypeStruct((slot_rows, head_dim), bf16),
        scratch_shapes=[
            pltpu.VMEM((slot_rows, head_dim), bf16),
            pltpu.VMEM((history, head_dim), bf16),
            pltpu.VMEM((history, head_dim), bf16),
            pltpu.VMEM((slot_rows, head_dim), bf16),
            pltpu.SemaphoreType.DMA((3 + slot_rows // block,)),
        ],
        compiler_params=roomy,
        name="history",
    )(
        my_index,
        session_slot,
        hist_len,
        got.reshape(slot_rows, head_dim),
        cache_keys.reshape(history, head_dim),
        cache_values.reshape(history, head_dim),
    )
    pieces, named_later, answers = lax.optimization_barrier((pieces, named, answers))
    for step in range(near + 1, half + 1):
        pieces[-step] = shifted(pieces[-near], step - near)
        if 2 * step < groups:
            pieces[step] = shifted(pieces[near], near - step)
    mine = pl.pallas_call(
        functools.partial(local_kernel, capacity, cands),
        in_specs=[VMEM] * 6,
        out_specs=HBM,
        out_shape=jax.ShapeDtypeStruct((rows, 3 * head_dim), f32),
        scratch_shapes=[pltpu.VMEM((rows, 3 * head_dim), f32), pltpu.SemaphoreType.DMA],
        compiler_params=params,
        cost_estimate=pl.CostEstimate(
            flops=2 * rows * model_width * 4 * head_dim, bytes_accessed=4 << 20, transcendentals=rows * 4 * head_dim
        ),
        name="local",
    )(tokens, w_flat, slots, named_later, counts, lengths)
    returned = lax.all_to_all(
        answers.reshape(replicas, capacity * cands, head_dim), "replica", split_axis=0, concat_axis=0, tiled=True
    )
    gated = pl.pallas_call(
        gate_kernel,
        in_specs=[ANY, HBM],
        out_specs=HBM,
        out_shape=jax.ShapeDtypeStruct((rows, head_dim), bf16),
        scratch_shapes=[
            pltpu.VMEM((slot_rows, head_dim), bf16),
            pltpu.VMEM((rows, 3 * head_dim), f32),
            pltpu.VMEM((rows, head_dim), bf16),
            pltpu.SemaphoreType.DMA((2,)),
        ],
        compiler_params=tight,
        name="gate",
    )(returned.reshape(slot_rows, head_dim), mine)
    share = rows // groups
    heads = lax.all_to_all(
        gated.reshape(groups, share, head_dim), "tensor", split_axis=0, concat_axis=0, tiled=True
    )
    return pl.pallas_call(
        output_kernel,
        in_specs=[SMEM, HBM] + [ANY] * (1 + groups),
        out_specs=HBM,
        out_shape=jax.ShapeDtypeStruct((share, model_width), bf16),
        scratch_shapes=[
            pltpu.VMEM((groups, share, head_dim), bf16),
            pltpu.VMEM((groups * head_dim, model_width), bf16),
            pltpu.VMEM((share, model_width), bf16),
            pltpu.VMEM((share, model_width), bf16),
            pltpu.SemaphoreType.DMA((groups + 2,)),
        ],
        compiler_params=tight,
        name="output",
    )(group_index, tokens, heads, *[pieces[shift] for shift in ring_order(groups)])


def solution(mesh):
    in_specs = (
        P("replica", None),
        P(None, "tensor", None),
        P("tensor", None, None),
        P("replica", None, "tensor", None),
        P("replica", None, "tensor", None),
        P(),
        P("replica"),
        P("replica"),
        P(),
    )
    out_specs = P(("replica", "tensor"), None)
    return jax.shard_map(
        on_device, mesh=mesh, in_specs=in_specs, out_specs=out_specs, check_vma=False
    )
```

```python
import functools

import jax
import jax.numpy as jnp
from jax import lax
from jax.experimental import pallas as pl
from jax.experimental.pallas import tpu as pltpu
from jax.sharding import PartitionSpec as P

epsilon = 1e-05
f32 = jnp.float32
bf16 = jnp.bfloat16


def layer_norm(values):
    average = jnp.mean(values, -1, keepdims=True)
    centred = values - average
    return centred * lax.rsqrt(jnp.mean(centred * centred, -1, keepdims=True) + epsilon)


def silu(values):
    half = values * 0.5
    return half + half * jnp.tanh(half)


def iota(shape, dimension):
    return lax.broadcasted_iota(jnp.int32, shape, dimension)


def to_column(row):
    n = row.shape[1]
    return jnp.sum(jnp.where(iota((n, n), 0) == iota((n, n), 1), row, 0.0), 1, keepdims=True)


def lookup(table_row, index_row):
    sessions, requests = table_row.shape[1], index_row.shape[1]
    named = iota((sessions, requests), 0) == index_row
    return jnp.sum(jnp.where(named, to_column(table_row.astype(f32)), 0.0), 0, keepdims=True)


def first_rows(slot_ref, session_ref, capacity, cands):
    owner = lookup(slot_ref[...], session_ref[...])
    requests = owner.shape[1]
    square = (requests, requests)
    earlier = (to_column(owner) == owner) & (iota(square, 0) < iota(square, 1))
    rank = jnp.sum(jnp.where(earlier, 1.0, 0.0), 0, keepdims=True)
    return (owner * capacity + rank) * cands


def send_kernel(
    capacity, cands, chunks, tokens_ref, w_ref, slot_ref, session_ref, sent_ref, held, weight, queries, placed, sems, w_sem, out_sems
):
    rows = tokens_ref.shape[0]
    head_dim = weight.shape[1]
    slot_rows = sent_ref.shape[0]
    chunk = rows // chunks
    fetch_w = pltpu.make_async_copy(w_ref.at[:, pl.ds(2 * head_dim, head_dim)], weight, w_sem)
    fetches = [
        pltpu.make_async_copy(
            tokens_ref.at[pl.ds(n * chunk, chunk), :], held.at[pl.ds(n * chunk, chunk), :], sems.at[n]
        )
        for n in range(chunks)
    ]
    fetches[0].start()
    fetch_w.start()
    for fetch in fetches[1:]:
        fetch.start()
    first = first_rows(slot_ref, session_ref, capacity, cands)
    requests = first.shape[1]
    spread = iota((requests, rows), 1) // cands == iota((requests, rows), 0)
    place = jnp.sum(jnp.where(spread, to_column(first), 0.0), 0, keepdims=True).astype(jnp.int32)
    place = place + iota((1, rows), 1) % cands
    for n, fetch in enumerate(fetches):
        part = pl.ds(n * chunk, chunk)
        fetch.wait()
        normed = layer_norm(held[part, :].astype(f32)).astype(bf16)
        if n == 0:
            fetch_w.wait()
        queries[part, :] = silu(jnp.dot(normed, weight[...], preferred_element_type=f32)).astype(bf16)
    block = slot_rows // chunks
    stores = []
    for n in range(chunks):
        part = pl.ds(n * block, block)
        chosen = jnp.where(iota((block, rows), 0) + n * block == place, 1.0, 0.0).astype(bf16)
        placed[part, :] = jnp.dot(chosen, queries[...], preferred_element_type=f32).astype(bf16)
        stores.append(pltpu.make_async_copy(placed.at[part, :], sent_ref.at[part, :], out_sems.at[n]))
        stores[-1].start()
    for store in stores:
        store.wait()


def local_kernel(
    capacity, cands, tokens_ref, w_ref, slot_ref, session_ref, count_ref, length_ref, out_ref, result, sem
):
    rows = tokens_ref.shape[0]
    head_dim = result.shape[1] // 3
    normed = layer_norm(tokens_ref[...].astype(f32)).astype(bf16)
    projected = silu(jnp.dot(normed, w_ref[...], preferred_element_type=f32)).astype(bf16).astype(f32)
    gate = projected[:, :head_dim]
    values = projected[:, head_dim : 2 * head_dim]
    queries = projected[:, 2 * head_dim : 3 * head_dim]
    keys = projected[:, 3 * head_dim :]
    lengths = lookup(length_ref[...], session_ref[...])
    requests = lengths.shape[1]
    spread = iota((rows, requests), 0) // cands == iota((rows, requests), 1)

    def per_row(row):
        return jnp.sum(jnp.where(spread, row, 0.0), 1, keepdims=True)

    within = (iota((rows, 1), 0) % cands).astype(f32)
    scores = jnp.sum(queries * keys, -1, keepdims=True) * head_dim ** (-0.5)
    result[:, :head_dim] = silu(scores) * values / (per_row(lengths) + 1.0)
    alive = within < per_row(count_ref[...].astype(f32))
    result[:, head_dim : 2 * head_dim] = jnp.where(alive, gate, 0.0)
    place = per_row(first_rows(slot_ref, session_ref, capacity, cands)) + within
    result[:, 2 * head_dim :] = jnp.broadcast_to(place, (rows, head_dim))
    store = pltpu.make_async_copy(result, out_ref, sem)
    store.start()
    store.wait()


def history_kernel(
    block, me_ref, slot_ref, length_ref, query_ref, keys_ref, values_ref, out_ref, query, keys, values, result, sems
):
    fetches = [
        pltpu.make_async_copy(source, target, sems.at[n])
        for n, (source, target) in enumerate(((keys_ref, keys), (query_ref, query), (values_ref, values)))
    ]
    for fetch in fetches:
        fetch.start()
    history, head_dim = keys_ref.shape
    length = jnp.zeros((), jnp.int32)
    for session in range(slot_ref.shape[0]):
        length = jnp.where(slot_ref[session] == me_ref[0], length_ref[session], length)
    seen = iota((history, 1), 0) < length
    divisor = (length + 1).astype(f32)
    half_scale = 0.5 * head_dim ** (-0.5)
    fetches[0].wait()
    fetches[1].wait()
    fetches[2].wait()
    seen_values = jnp.where(seen, values[...], jnp.zeros((), bf16))
    stores = []
    for n, start in enumerate(range(0, query_ref.shape[0], block)):
        part = pl.ds(start, block)
        half = (
            lax.dot_general(query[part, :], keys[...], (((1,), (1,)), ((), ())), preferred_element_type=f32)
            * half_scale
        )
        weights = (half + half * jnp.tanh(half)).astype(bf16)
        summed = jnp.dot(weights, seen_values, preferred_element_type=f32)
        result[part, :] = (summed / divisor).astype(bf16)
        stores.append(pltpu.make_async_copy(result.at[part, :], out_ref.at[part, :], sems.at[3 + n]))
        stores[-1].start()
    for store in stores:
        store.wait()


def gate_kernel(returned_ref, mine_ref, out_ref, returned, mine, result, sems):
    fetches = [
        pltpu.make_async_copy(mine_ref, mine, sems.at[0]),
        pltpu.make_async_copy(returned_ref, returned, sems.at[1]),
    ]
    for fetch in fetches:
        fetch.start()
    rows, head_dim = result.shape
    slot_rows = returned.shape[0]
    fetches[0].wait()
    place = mine[:, 2 * head_dim : 2 * head_dim + 1].astype(jnp.int32)
    back = jnp.where(iota((rows, slot_rows), 1) == place, 1.0, 0.0).astype(bf16)
    fetches[1].wait()
    part = jnp.dot(back, returned[...], preferred_element_type=f32)
    result[...] = (layer_norm(part + mine[:, :head_dim]) * mine[:, head_dim : 2 * head_dim]).astype(bf16)
    store = pltpu.make_async_copy(result, out_ref, sems.at[0])
    store.start()
    store.wait()


held_heads = ((0, 1), (2, 3), (4, -1), (-2, -3))


def output_kernel(
    group_ref, me_ref, tokens_ref, gated_ref, own_ref, one_ref, two_ref, last_ref, other_one_ref, other_two_ref,
    out_ref, gated, weight, tokens, result, sems,
):
    groups, share, head_dim = gated_ref.shape
    group = group_ref[0]
    sign = jnp.where(me_ref[0] % 2 == 0, -1, 1)
    fetches = [pltpu.make_async_copy(gated_ref, gated, sems.at[0])]
    start = 0
    for n, piece in enumerate((own_ref, one_ref, two_ref, last_ref, other_one_ref, other_two_ref)):
        size = piece.shape[0]
        fetches.append(pltpu.make_async_copy(piece, weight.at[pl.ds(start, size), :], sems.at[1 + n]))
        start += size
    mine = pl.ds(pl.multiple_of(group * share, share), share)
    fetch_tokens = pltpu.make_async_copy(tokens_ref.at[mine, :], tokens, sems.at[7])
    for fetch in fetches:
        fetch.start()
    fetch_tokens.start()
    total = jnp.zeros(result.shape, f32)
    fetches[0].wait()
    for n, heads in enumerate(held_heads):
        for fetch in (fetches[1:3], fetches[3:4], fetches[4:6], fetches[6:7])[n]:
            fetch.wait()
        pair = jnp.concatenate(
            [gated[lax.rem(group + sign * head + groups, groups)] for head in heads], axis=1
        )
        total = total + jnp.dot(
            pair, weight[pl.ds(2 * n * head_dim, 2 * head_dim), :], preferred_element_type=f32
        )
    fetch_tokens.wait()
    result[...] = (tokens[...].astype(f32) + total).astype(bf16)
    store = pltpu.make_async_copy(result, out_ref, sems.at[0])
    store.start()
    store.wait()


ANY = pl.BlockSpec(memory_space=pl.ANY)
HBM = pl.BlockSpec(memory_space=pltpu.HBM)
VMEM = pl.BlockSpec(memory_space=pltpu.VMEM)
SMEM = pl.BlockSpec(memory_space=pltpu.SMEM)
params = pltpu.CompilerParams(vmem_limit_bytes=63 * 1024 * 1024)
tight = pltpu.CompilerParams(vmem_limit_bytes=54528 * 1024)
roomy = pltpu.CompilerParams(vmem_limit_bytes=24 * 1024 * 1024)


def on_device(
    tokens,
    w_in,
    w_out,
    cache_keys,
    cache_values,
    session_slot,
    request_session,
    cand_count,
    hist_len,
):
    replicas = lax.axis_size("replica")
    groups = lax.axis_size("tensor")
    my_index = lax.axis_index("replica").astype(jnp.int32).reshape(1)
    group_index = lax.axis_index("tensor").astype(jnp.int32).reshape(1)
    rows, model_width = tokens.shape
    head_dim = w_in.shape[2] // 4
    requests = request_session.shape[0]
    cands = rows // requests
    history = cache_keys.shape[1]
    capacity = max(2, (2 * requests + replicas - 1) // replicas)
    slot_rows = replicas * capacity * cands
    w_flat = w_in.reshape(model_width, 4 * head_dim)
    slots = session_slot.reshape(1, -1)
    lengths = hist_len.reshape(1, -1)
    named = request_session.reshape(1, -1)
    counts = cand_count.reshape(1, -1)
    chunks = 4

    sent = pl.pallas_call(
        functools.partial(send_kernel, capacity, cands, chunks),
        in_specs=[HBM, HBM, VMEM, VMEM],
        out_specs=HBM,
        out_shape=jax.ShapeDtypeStruct((slot_rows, head_dim), bf16),
        scratch_shapes=[
            pltpu.VMEM((rows, model_width), bf16),
            pltpu.VMEM((model_width, head_dim), bf16),
            pltpu.VMEM((rows, head_dim), bf16),
            pltpu.VMEM((slot_rows, head_dim), bf16),
            pltpu.SemaphoreType.DMA((chunks,)),
            pltpu.SemaphoreType.DMA,
            pltpu.SemaphoreType.DMA((chunks,)),
        ],
        compiler_params=params,
        name="send",
    )(tokens, w_flat, slots, named)
    got = lax.all_to_all(
        sent.reshape(replicas, capacity * cands, head_dim), "replica", split_axis=0, concat_axis=0, tiled=True
    )
    def passed(piece, by):
        pairs = []
        for r in range(replicas):
            for z in range(groups):
                pairs.append((r * groups + z, r * groups + (z + (by if r % 2 == 0 else -by)) % groups))
        return lax.ppermute(piece, ("replica", "tensor"), pairs)

    def swapped(piece):
        return lax.ppermute(piece, "replica", [(r, r ^ 1) for r in range(replicas)])

    w_own = w_out.reshape(head_dim, model_width)
    next_one = passed(w_own, 1)
    w_own, next_one, sent = lax.optimization_barrier((w_own, next_one, sent))
    next_two = passed(jnp.concatenate([w_own, next_one], axis=0), 2)
    other_one = swapped(next_one)
    block = min(256, slot_rows)
    answers = pl.pallas_call(
        functools.partial(history_kernel, block),
        in_specs=[SMEM, SMEM, SMEM, ANY, HBM, HBM],
        out_specs=HBM,
        out_shape=jax.ShapeDtypeStruct((slot_rows, head_dim), bf16),
        scratch_shapes=[
            pltpu.VMEM((slot_rows, head_dim), bf16),
            pltpu.VMEM((history, head_dim), bf16),
            pltpu.VMEM((history, head_dim), bf16),
            pltpu.VMEM((slot_rows, head_dim), bf16),
            pltpu.SemaphoreType.DMA((3 + slot_rows // block,)),
        ],
        compiler_params=roomy,
        cost_estimate=pl.CostEstimate(flops=1 << 30, bytes_accessed=64 << 20, transcendentals=slot_rows * history),
        name="history",
    )(
        my_index,
        session_slot,
        hist_len,
        got.reshape(slot_rows, head_dim),
        cache_keys.reshape(history, head_dim),
        cache_values.reshape(history, head_dim),
    )
    next_two, other_one, named_later, answers = lax.optimization_barrier((next_two, other_one, named, answers))
    last = passed(next_two[head_dim:], 1)
    other_two = swapped(next_two)
    mine = pl.pallas_call(
        functools.partial(local_kernel, capacity, cands),
        in_specs=[VMEM] * 6,
        out_specs=HBM,
        out_shape=jax.ShapeDtypeStruct((rows, 3 * head_dim), f32),
        scratch_shapes=[pltpu.VMEM((rows, 3 * head_dim), f32), pltpu.SemaphoreType.DMA],
        compiler_params=params,
        cost_estimate=pl.CostEstimate(
            flops=2 * rows * model_width * 4 * head_dim, bytes_accessed=4 << 20, transcendentals=rows * 4 * head_dim
        ),
        name="local",
    )(tokens, w_flat, slots, named_later, counts, lengths)
    returned = lax.all_to_all(
        answers.reshape(replicas, capacity * cands, head_dim), "replica", split_axis=0, concat_axis=0, tiled=True
    )
    gated = pl.pallas_call(
        gate_kernel,
        in_specs=[ANY, HBM],
        out_specs=HBM,
        out_shape=jax.ShapeDtypeStruct((rows, head_dim), bf16),
        scratch_shapes=[
            pltpu.VMEM((slot_rows, head_dim), bf16),
            pltpu.VMEM((rows, 3 * head_dim), f32),
            pltpu.VMEM((rows, head_dim), bf16),
            pltpu.SemaphoreType.DMA((2,)),
        ],
        compiler_params=tight,
        name="gate",
    )(returned.reshape(slot_rows, head_dim), mine)
    share = rows // groups
    heads = lax.all_to_all(
        gated.reshape(groups, share, head_dim), "tensor", split_axis=0, concat_axis=0, tiled=True
    )
    return pl.pallas_call(
        output_kernel,
        in_specs=[SMEM, SMEM, HBM] + [ANY] * 7,
        out_specs=HBM,
        out_shape=jax.ShapeDtypeStruct((share, model_width), bf16),
        scratch_shapes=[
            pltpu.VMEM((groups, share, head_dim), bf16),
            pltpu.VMEM((groups * head_dim, model_width), bf16),
            pltpu.VMEM((share, model_width), bf16),
            pltpu.VMEM((share, model_width), bf16),
            pltpu.SemaphoreType.DMA((8,)),
        ],
        compiler_params=tight,
        name="output",
    )(group_index, my_index, tokens, heads, w_own, next_one, next_two, last, other_one, other_two)


def solution(mesh):
    in_specs = (
        P("replica", None),
        P(None, "tensor", None),
        P("tensor", None, None),
        P("replica", None, "tensor", None),
        P("replica", None, "tensor", None),
        P(),
        P("replica"),
        P("replica"),
        P(),
    )
    out_specs = P(("replica", "tensor"), None)
    return jax.shard_map(
        on_device, mesh=mesh, in_specs=in_specs, out_specs=out_specs, check_vma=False
    )
```

```python
import functools

import jax
import jax.numpy as jnp
from jax import lax
from jax.experimental import pallas as pl
from jax.experimental.pallas import tpu as pltpu
from jax.sharding import PartitionSpec as P

epsilon = 1e-05
f32 = jnp.float32
bf16 = jnp.bfloat16


def layer_norm(values):
    average = jnp.mean(values, -1, keepdims=True)
    centred = values - average
    return centred * lax.rsqrt(jnp.mean(centred * centred, -1, keepdims=True) + epsilon)


def silu(values):
    half = values * 0.5
    return half + half * jnp.tanh(half)


def iota(shape, dimension):
    return lax.broadcasted_iota(jnp.int32, shape, dimension)


def to_column(row):
    n = row.shape[1]
    return jnp.sum(jnp.where(iota((n, n), 0) == iota((n, n), 1), row, 0.0), 1, keepdims=True)


def lookup(table_row, index_row):
    sessions, requests = table_row.shape[1], index_row.shape[1]
    named = iota((sessions, requests), 0) == index_row
    return jnp.sum(jnp.where(named, to_column(table_row.astype(f32)), 0.0), 0, keepdims=True)


def first_rows(slot_ref, session_ref, capacity, cands):
    owner = lookup(slot_ref[...], session_ref[...])
    requests = owner.shape[1]
    square = (requests, requests)
    earlier = (to_column(owner) == owner) & (iota(square, 0) < iota(square, 1))
    rank = jnp.sum(jnp.where(earlier, 1.0, 0.0), 0, keepdims=True)
    return (owner * capacity + rank) * cands


def send_kernel(
    capacity, cands, chunks, tokens_ref, w_ref, slot_ref, session_ref, length_ref, me_ref, sent_ref, info_ref,
    held, weight, queries, placed, info, sems, w_sem, out_sems,
):
    rows = tokens_ref.shape[0]
    head_dim = weight.shape[1]
    slot_rows = sent_ref.shape[0]
    chunk = rows // chunks
    fetch_w = pltpu.make_async_copy(w_ref.at[:, pl.ds(2 * head_dim, head_dim)], weight, w_sem)
    fetches = [
        pltpu.make_async_copy(
            tokens_ref.at[pl.ds(n * chunk, chunk), :], held.at[pl.ds(n * chunk, chunk), :], sems.at[n]
        )
        for n in range(chunks)
    ]
    fetches[0].start()
    fetch_w.start()
    for fetch in fetches[1:]:
        fetch.start()
    own = slot_ref[...] == me_ref[0]
    length = jnp.sum(jnp.where(own, length_ref[...].astype(f32), 0.0), 1, keepdims=True)
    info[...] = jnp.broadcast_to(length, info.shape)
    stores = [pltpu.make_async_copy(info, info_ref, out_sems.at[chunks])]
    stores[0].start()
    first = first_rows(slot_ref, session_ref, capacity, cands)
    requests = first.shape[1]
    spread = iota((requests, rows), 1) // cands == iota((requests, rows), 0)
    place = jnp.sum(jnp.where(spread, to_column(first), 0.0), 0, keepdims=True).astype(jnp.int32)
    place = place + iota((1, rows), 1) % cands
    for n, fetch in enumerate(fetches):
        part = pl.ds(n * chunk, chunk)
        fetch.wait()
        normed = layer_norm(held[part, :].astype(f32)).astype(bf16)
        if n == 0:
            fetch_w.wait()
        queries[part, :] = silu(jnp.dot(normed, weight[...], preferred_element_type=f32)).astype(bf16)
    block = slot_rows // chunks
    for n in range(chunks):
        part = pl.ds(n * block, block)
        chosen = jnp.where(iota((block, rows), 0) + n * block == place, 1.0, 0.0).astype(bf16)
        placed[part, :] = jnp.dot(chosen, queries[...], preferred_element_type=f32).astype(bf16)
        stores.append(pltpu.make_async_copy(placed.at[part, :], sent_ref.at[part, :], out_sems.at[n]))
        stores[-1].start()
    for store in stores:
        store.wait()


def local_kernel(
    capacity, cands, tokens_ref, w_ref, slot_ref, session_ref, count_ref, length_ref, out_ref, result, sem
):
    rows = tokens_ref.shape[0]
    head_dim = result.shape[1] // 3
    normed = layer_norm(tokens_ref[...].astype(f32)).astype(bf16)
    projected = silu(jnp.dot(normed, w_ref[...], preferred_element_type=f32)).astype(bf16).astype(f32)
    gate = projected[:, :head_dim]
    values = projected[:, head_dim : 2 * head_dim]
    queries = projected[:, 2 * head_dim : 3 * head_dim]
    keys = projected[:, 3 * head_dim :]
    lengths = lookup(length_ref[...], session_ref[...])
    requests = lengths.shape[1]
    spread = iota((rows, requests), 0) // cands == iota((rows, requests), 1)

    def per_row(row):
        return jnp.sum(jnp.where(spread, row, 0.0), 1, keepdims=True)

    within = (iota((rows, 1), 0) % cands).astype(f32)
    scores = jnp.sum(queries * keys, -1, keepdims=True) * head_dim ** (-0.5)
    result[:, :head_dim] = silu(scores) * values / (per_row(lengths) + 1.0)
    alive = within < per_row(count_ref[...].astype(f32))
    result[:, head_dim : 2 * head_dim] = jnp.where(alive, gate, 0.0)
    place = per_row(first_rows(slot_ref, session_ref, capacity, cands)) + within
    result[:, 2 * head_dim :] = jnp.broadcast_to(place, (rows, head_dim))
    store = pltpu.make_async_copy(result, out_ref, sem)
    store.start()
    store.wait()


def history_kernel(
    block, info_ref, query_ref, keys_ref, values_ref, out_ref, info, query, keys, values, result, sems
):
    fetches = [
        pltpu.make_async_copy(source, target, sems.at[n])
        for n, (source, target) in enumerate(
            ((info_ref, info), (query_ref, query), (keys_ref, keys), (values_ref, values))
        )
    ]
    for fetch in fetches:
        fetch.start()
    history, head_dim = keys_ref.shape
    half_scale = 0.5 * head_dim ** (-0.5)
    for fetch in fetches:
        fetch.wait()
    length = info[:1, :1]
    divisor = length + 1.0
    seen = iota((history, 1), 0).astype(f32) < length
    seen_values = jnp.where(seen, values[...], jnp.zeros((), bf16))
    stores = []
    for n, start in enumerate(range(0, query_ref.shape[0], block)):
        part = pl.ds(start, block)
        half = (
            lax.dot_general(query[part, :], keys[...], (((1,), (1,)), ((), ())), preferred_element_type=f32)
            * half_scale
        )
        weights = (half + half * jnp.tanh(half)).astype(bf16)
        summed = jnp.dot(weights, seen_values, preferred_element_type=f32)
        result[part, :] = (summed / divisor).astype(bf16)
        stores.append(pltpu.make_async_copy(result.at[part, :], out_ref.at[part, :], sems.at[4 + n]))
        stores[-1].start()
    for store in stores:
        store.wait()


def gate_kernel(returned_ref, mine_ref, out_ref, returned, mine, result, sems):
    fetches = [
        pltpu.make_async_copy(mine_ref, mine, sems.at[0]),
        pltpu.make_async_copy(returned_ref, returned, sems.at[1]),
    ]
    for fetch in fetches:
        fetch.start()
    rows, head_dim = result.shape
    slot_rows = returned.shape[0]
    fetches[0].wait()
    place = mine[:, 2 * head_dim : 2 * head_dim + 1].astype(jnp.int32)
    back = jnp.where(iota((rows, slot_rows), 1) == place, 1.0, 0.0).astype(bf16)
    fetches[1].wait()
    part = jnp.dot(back, returned[...], preferred_element_type=f32)
    result[...] = (layer_norm(part + mine[:, :head_dim]) * mine[:, head_dim : 2 * head_dim]).astype(bf16)
    store = pltpu.make_async_copy(result, out_ref, sems.at[0])
    store.start()
    store.wait()


held_heads = ((0, 1), (2, 3), (4, -1), (-2, -3))


def output_kernel(
    group_ref, me_ref, tokens_ref, gated_ref, own_ref, next_ref, last_ref, other_ref,
    out_ref, gated, weight, tokens, result, sems,
):
    groups, share, head_dim = gated_ref.shape
    group = group_ref[0]
    sign = jnp.where(me_ref[0] % 2 == 0, -1, 1)
    double = 2 * head_dim
    fetches = [pltpu.make_async_copy(gated_ref, gated, sems.at[0])]
    start = 0
    for n, source in enumerate((own_ref, next_ref, last_ref, other_ref)):
        size = source.shape[0]
        fetches.append(pltpu.make_async_copy(source, weight.at[pl.ds(start, size), :], sems.at[1 + n]))
        start += size
    mine = pl.ds(pl.multiple_of(group * share, share), share)
    fetch_tokens = pltpu.make_async_copy(tokens_ref.at[mine, :], tokens, sems.at[5])
    for fetch in fetches:
        fetch.start()
    fetch_tokens.start()
    total = jnp.zeros(result.shape, f32)
    for pair, waits in enumerate((fetches[:3], (), fetches[3:], ())):
        for fetch in waits:
            fetch.wait()
        rows = jnp.concatenate(
            [gated[lax.rem(group + sign * head + groups, groups)] for head in held_heads[pair]], axis=1
        )
        total = total + jnp.dot(rows, weight[pl.ds(pair * double, double), :], preferred_element_type=f32)
    fetch_tokens.wait()
    result[...] = (tokens[...].astype(f32) + total).astype(bf16)
    store = pltpu.make_async_copy(result, out_ref, sems.at[0])
    store.start()
    store.wait()


ANY = pl.BlockSpec(memory_space=pl.ANY)
HBM = pl.BlockSpec(memory_space=pltpu.HBM)
VMEM = pl.BlockSpec(memory_space=pltpu.VMEM)
SMEM = pl.BlockSpec(memory_space=pltpu.SMEM)
params = pltpu.CompilerParams(vmem_limit_bytes=63 * 1024 * 1024)
tight = pltpu.CompilerParams(vmem_limit_bytes=54528 * 1024)
roomy = pltpu.CompilerParams(vmem_limit_bytes=24 * 1024 * 1024)


def after(value, other):
    return lax.optimization_barrier((value, other))[0]


def on_device(
    tokens,
    w_in,
    w_out,
    cache_keys,
    cache_values,
    session_slot,
    request_session,
    cand_count,
    hist_len,
):
    replicas = lax.axis_size("replica")
    groups = lax.axis_size("tensor")
    my_index = lax.axis_index("replica").astype(jnp.int32).reshape(1)
    group_index = lax.axis_index("tensor").astype(jnp.int32).reshape(1)
    rows, model_width = tokens.shape
    head_dim = w_in.shape[2] // 4
    requests = request_session.shape[0]
    cands = rows // requests
    history = cache_keys.shape[1]
    capacity = max(2, (2 * requests + replicas - 1) // replicas)
    slot_rows = replicas * capacity * cands
    w_flat = w_in.reshape(model_width, 4 * head_dim)
    slots = session_slot.reshape(1, -1)
    lengths = hist_len.reshape(1, -1)
    named = request_session.reshape(1, -1)
    counts = cand_count.reshape(1, -1)
    chunks = 4

    sent, info = pl.pallas_call(
        functools.partial(send_kernel, capacity, cands, chunks),
        in_specs=[HBM, HBM, VMEM, VMEM, VMEM, SMEM],
        out_specs=[HBM, HBM],
        out_shape=[jax.ShapeDtypeStruct((slot_rows, head_dim), bf16), jax.ShapeDtypeStruct((8, 128), f32)],
        scratch_shapes=[
            pltpu.VMEM((rows, model_width), bf16),
            pltpu.VMEM((model_width, head_dim), bf16),
            pltpu.VMEM((rows, head_dim), bf16),
            pltpu.VMEM((slot_rows, head_dim), bf16),
            pltpu.VMEM((8, 128), f32),
            pltpu.SemaphoreType.DMA((chunks,)),
            pltpu.SemaphoreType.DMA,
            pltpu.SemaphoreType.DMA((chunks + 1,)),
        ],
        compiler_params=params,
        name="send",
    )(tokens, w_flat, slots, named, lengths, my_index)
    got = lax.all_to_all(
        sent.reshape(replicas, capacity * cands, head_dim), "replica", split_axis=0, concat_axis=0, tiled=True
    )
    def passed(piece, by):
        pairs = []
        for r in range(replicas):
            for z in range(groups):
                pairs.append((r * groups + z, r * groups + (z + (by if r % 2 == 0 else -by)) % groups))
        return lax.ppermute(piece, ("replica", "tensor"), pairs)

    def swapped(piece):
        return lax.ppermute(piece, "replica", [(r, r ^ 1) for r in range(replicas)])

    w_own = after(w_out.reshape(head_dim, model_width), sent)
    nexts = [passed(w_own, by) for by in range(1, groups // 2)]
    block = min(256, slot_rows)
    answers = pl.pallas_call(
        functools.partial(history_kernel, block),
        in_specs=[HBM, ANY, HBM, HBM],
        out_specs=HBM,
        out_shape=jax.ShapeDtypeStruct((slot_rows, head_dim), bf16),
        scratch_shapes=[
            pltpu.VMEM((8, 128), f32),
            pltpu.VMEM((slot_rows, head_dim), bf16),
            pltpu.VMEM((history, head_dim), bf16),
            pltpu.VMEM((history, head_dim), bf16),
            pltpu.VMEM((slot_rows, head_dim), bf16),
            pltpu.SemaphoreType.DMA((4 + slot_rows // block,)),
        ],
        compiler_params=tight,
        cost_estimate=pl.CostEstimate(flops=1 << 30, bytes_accessed=64 << 20, transcendentals=slot_rows * history),
        name="history",
    )(
        info,
        got.reshape(slot_rows, head_dim),
        cache_keys.reshape(history, head_dim),
        cache_values.reshape(history, head_dim),
    )
    nexts = jnp.concatenate([after(piece, answers) for piece in nexts], axis=0)
    last = passed(nexts[-head_dim:], 1)
    others = swapped(nexts)
    mine = pl.pallas_call(
        functools.partial(local_kernel, capacity, cands),
        in_specs=[VMEM] * 6,
        out_specs=HBM,
        out_shape=jax.ShapeDtypeStruct((rows, 3 * head_dim), f32),
        scratch_shapes=[pltpu.VMEM((rows, 3 * head_dim), f32), pltpu.SemaphoreType.DMA],
        compiler_params=params,
        cost_estimate=pl.CostEstimate(flops=1 << 30, bytes_accessed=16 << 20, transcendentals=1 << 18),
        name="local",
    )(tokens, w_flat, slots, after(named, answers), counts, lengths)
    returned = lax.all_to_all(
        answers.reshape(replicas, capacity * cands, head_dim), "replica", split_axis=0, concat_axis=0, tiled=True
    )
    gated = pl.pallas_call(
        gate_kernel,
        in_specs=[ANY, HBM],
        out_specs=HBM,
        out_shape=jax.ShapeDtypeStruct((rows, head_dim), bf16),
        scratch_shapes=[
            pltpu.VMEM((slot_rows, head_dim), bf16),
            pltpu.VMEM((rows, 3 * head_dim), f32),
            pltpu.VMEM((rows, head_dim), bf16),
            pltpu.SemaphoreType.DMA((2,)),
        ],
        compiler_params=tight,
        cost_estimate=pl.CostEstimate(flops=1 << 30, bytes_accessed=64 << 20, transcendentals=1 << 10),
        name="gate",
    )(returned.reshape(slot_rows, head_dim), mine)
    share = rows // groups
    heads = lax.all_to_all(
        gated.reshape(groups, share, head_dim), "tensor", split_axis=0, concat_axis=0, tiled=True
    )
    return pl.pallas_call(
        output_kernel,
        in_specs=[SMEM, SMEM, HBM] + [ANY] * 5,
        out_specs=HBM,
        out_shape=jax.ShapeDtypeStruct((share, model_width), bf16),
        scratch_shapes=[
            pltpu.VMEM((groups, share, head_dim), bf16),
            pltpu.VMEM((groups * head_dim, model_width), bf16),
            pltpu.VMEM((share, model_width), bf16),
            pltpu.VMEM((share, model_width), bf16),
            pltpu.SemaphoreType.DMA((6,)),
        ],
        compiler_params=tight,
        name="output",
    )(group_index, my_index, tokens, heads, w_own, nexts, last, others)


def solution(mesh):
    in_specs = (
        P("replica", None),
        P(None, "tensor", None),
        P("tensor", None, None),
        P("replica", None, "tensor", None),
        P("replica", None, "tensor", None),
        P(),
        P("replica"),
        P("replica"),
        P(),
    )
    out_specs = P(("replica", "tensor"), None)
    return jax.shard_map(
        on_device, mesh=mesh, in_specs=in_specs, out_specs=out_specs, check_vma=False
    )
```

```python
import functools

import jax
import jax.numpy as jnp
from jax import lax
from jax.experimental import pallas as pl
from jax.experimental.pallas import tpu as pltpu
from jax.sharding import PartitionSpec as P

epsilon = 1e-05
f32 = jnp.float32
bf16 = jnp.bfloat16


def layer_norm(values):
    average = jnp.mean(values, -1, keepdims=True)
    centred = values - average
    return centred * lax.rsqrt(jnp.mean(centred * centred, -1, keepdims=True) + epsilon)


def silu(values):
    half = values * 0.5
    return half + half * jnp.tanh(half)


def iota(shape, dimension):
    return lax.broadcasted_iota(jnp.int32, shape, dimension)


def to_column(row):
    n = row.shape[1]
    return jnp.sum(jnp.where(iota((n, n), 0) == iota((n, n), 1), row, 0.0), 1, keepdims=True)


def lookup(table_row, index_row):
    sessions, requests = table_row.shape[1], index_row.shape[1]
    named = iota((sessions, requests), 0) == index_row
    return jnp.sum(jnp.where(named, to_column(table_row.astype(f32)), 0.0), 0, keepdims=True)


def first_rows(slot_ref, session_ref, capacity, cands):
    owner = lookup(slot_ref[...], session_ref[...])
    requests = owner.shape[1]
    square = (requests, requests)
    earlier = (to_column(owner) == owner) & (iota(square, 0) < iota(square, 1))
    rank = jnp.sum(jnp.where(earlier, 1.0, 0.0), 0, keepdims=True)
    return (owner * capacity + rank) * cands


def send_kernel(
    capacity, cands, chunks, tokens_ref, w_ref, slot_ref, session_ref, length_ref, me_ref, sent_ref, info_ref,
    held, weight, queries, placed, info, sems, w_sem, out_sems,
):
    rows = tokens_ref.shape[0]
    head_dim = weight.shape[1]
    slot_rows = sent_ref.shape[0]
    chunk = rows // chunks
    fetch_w = pltpu.make_async_copy(w_ref.at[:, pl.ds(2 * head_dim, head_dim)], weight, w_sem)
    fetches = [
        pltpu.make_async_copy(
            tokens_ref.at[pl.ds(n * chunk, chunk), :], held.at[pl.ds(n * chunk, chunk), :], sems.at[n]
        )
        for n in range(chunks)
    ]
    fetches[0].start()
    fetch_w.start()
    for fetch in fetches[1:]:
        fetch.start()
    own = slot_ref[...] == me_ref[0]
    length = jnp.sum(jnp.where(own, length_ref[...].astype(f32), 0.0), 1, keepdims=True)
    info[...] = jnp.broadcast_to(length, info.shape)
    stores = [pltpu.make_async_copy(info, info_ref, out_sems.at[chunks])]
    stores[0].start()
    first = first_rows(slot_ref, session_ref, capacity, cands)
    requests = first.shape[1]
    spread = iota((requests, rows), 1) // cands == iota((requests, rows), 0)
    place = jnp.sum(jnp.where(spread, to_column(first), 0.0), 0, keepdims=True).astype(jnp.int32)
    place = place + iota((1, rows), 1) % cands
    for n, fetch in enumerate(fetches):
        part = pl.ds(n * chunk, chunk)
        fetch.wait()
        normed = layer_norm(held[part, :].astype(f32)).astype(bf16)
        if n == 0:
            fetch_w.wait()
        queries[part, :] = silu(jnp.dot(normed, weight[...], preferred_element_type=f32)).astype(bf16)
    block = slot_rows // chunks
    for n in range(chunks):
        part = pl.ds(n * block, block)
        chosen = jnp.where(iota((block, rows), 0) + n * block == place, 1.0, 0.0).astype(bf16)
        placed[part, :] = jnp.dot(chosen, queries[...], preferred_element_type=f32).astype(bf16)
        stores.append(pltpu.make_async_copy(placed.at[part, :], sent_ref.at[part, :], out_sems.at[n]))
        stores[-1].start()
    for store in stores:
        store.wait()


def local_kernel(
    capacity, cands, tokens_ref, w_ref, slot_ref, session_ref, count_ref, length_ref, out_ref, result, sem
):
    rows = tokens_ref.shape[0]
    head_dim = result.shape[1] // 3
    normed = layer_norm(tokens_ref[...].astype(f32)).astype(bf16)
    projected = silu(jnp.dot(normed, w_ref[...], preferred_element_type=f32)).astype(bf16).astype(f32)
    gate = projected[:, :head_dim]
    values = projected[:, head_dim : 2 * head_dim]
    queries = projected[:, 2 * head_dim : 3 * head_dim]
    keys = projected[:, 3 * head_dim :]
    lengths = lookup(length_ref[...], session_ref[...])
    requests = lengths.shape[1]
    spread = iota((rows, requests), 0) // cands == iota((rows, requests), 1)

    def per_row(row):
        return jnp.sum(jnp.where(spread, row, 0.0), 1, keepdims=True)

    within = (iota((rows, 1), 0) % cands).astype(f32)
    scores = jnp.sum(queries * keys, -1, keepdims=True) * head_dim ** (-0.5)
    result[:, :head_dim] = silu(scores) * values / (per_row(lengths) + 1.0)
    alive = within < per_row(count_ref[...].astype(f32))
    result[:, head_dim : 2 * head_dim] = jnp.where(alive, gate, 0.0)
    place = per_row(first_rows(slot_ref, session_ref, capacity, cands)) + within
    result[:, 2 * head_dim :] = jnp.broadcast_to(place, (rows, head_dim))
    store = pltpu.make_async_copy(result, out_ref, sem)
    store.start()
    store.wait()


def history_kernel(
    block, info_ref, query_ref, keys_ref, values_ref, out_ref, info, query, keys, values, result, sems
):
    fetches = [
        pltpu.make_async_copy(source, target, sems.at[n])
        for n, (source, target) in enumerate(
            ((info_ref, info), (query_ref, query), (keys_ref, keys), (values_ref, values))
        )
    ]
    for fetch in fetches:
        fetch.start()
    history, head_dim = keys_ref.shape
    half_scale = 0.5 * head_dim ** (-0.5)
    for fetch in fetches:
        fetch.wait()
    length = info[:1, :1]
    divisor = length + 1.0
    seen = iota((history, 1), 0).astype(f32) < length
    seen_values = jnp.where(seen, values[...], jnp.zeros((), bf16))
    stores = []
    for n, start in enumerate(range(0, query_ref.shape[0], block)):
        part = pl.ds(start, block)
        half = (
            lax.dot_general(query[part, :], keys[...], (((1,), (1,)), ((), ())), preferred_element_type=f32)
            * half_scale
        )
        weights = (half + half * jnp.tanh(half)).astype(bf16)
        summed = jnp.dot(weights, seen_values, preferred_element_type=f32)
        result[part, :] = (summed / divisor).astype(bf16)
        stores.append(pltpu.make_async_copy(result.at[part, :], out_ref.at[part, :], sems.at[4 + n]))
        stores[-1].start()
    for store in stores:
        store.wait()


def gate_kernel(returned_ref, mine_ref, out_ref, returned, mine, result, sems):
    fetches = [
        pltpu.make_async_copy(mine_ref, mine, sems.at[0]),
        pltpu.make_async_copy(returned_ref, returned, sems.at[1]),
    ]
    for fetch in fetches:
        fetch.start()
    rows, head_dim = result.shape
    slot_rows = returned.shape[0]
    fetches[0].wait()
    place = mine[:, 2 * head_dim : 2 * head_dim + 1].astype(jnp.int32)
    back = jnp.where(iota((rows, slot_rows), 1) == place, 1.0, 0.0).astype(bf16)
    fetches[1].wait()
    part = jnp.dot(back, returned[...], preferred_element_type=f32)
    result[...] = (layer_norm(part + mine[:, :head_dim]) * mine[:, head_dim : 2 * head_dim]).astype(bf16)
    store = pltpu.make_async_copy(result, out_ref, sems.at[0])
    store.start()
    store.wait()


held_heads = ((0, 1), (2, 3), (4, -1), (-2, -3))


def output_kernel(
    group_ref, me_ref, tokens_ref, gated_ref, own_ref, next_ref, last_ref, other_ref, three_ref,
    out_ref, gated, weight, tokens, result, sems,
):
    groups, share, head_dim = gated_ref.shape
    group = group_ref[0]
    sign = jnp.where(me_ref[0] % 2 == 0, -1, 1)
    double = 2 * head_dim
    fetches = [pltpu.make_async_copy(gated_ref, gated, sems.at[0])]
    start = 0
    for n, source in enumerate((own_ref, next_ref, last_ref, other_ref, three_ref)):
        size = source.shape[0]
        fetches.append(pltpu.make_async_copy(source, weight.at[pl.ds(start, size), :], sems.at[1 + n]))
        start += size
    mine = pl.ds(pl.multiple_of(group * share, share), share)
    fetch_tokens = pltpu.make_async_copy(tokens_ref.at[mine, :], tokens, sems.at[6])
    for fetch in fetches:
        fetch.start()
    fetch_tokens.start()
    total = jnp.zeros(result.shape, f32)
    for pair, waits in enumerate((fetches[:3], fetches[3:4], fetches[4:5], fetches[5:])):
        for fetch in waits:
            fetch.wait()
        rows = jnp.concatenate(
            [gated[lax.rem(group + sign * head + groups, groups)] for head in held_heads[pair]], axis=1
        )
        total = total + jnp.dot(rows, weight[pl.ds(pair * double, double), :], preferred_element_type=f32)
    fetch_tokens.wait()
    result[...] = (tokens[...].astype(f32) + total).astype(bf16)
    store = pltpu.make_async_copy(result, out_ref, sems.at[0])
    store.start()
    store.wait()


ANY = pl.BlockSpec(memory_space=pl.ANY)
HBM = pl.BlockSpec(memory_space=pltpu.HBM)
VMEM = pl.BlockSpec(memory_space=pltpu.VMEM)
SMEM = pl.BlockSpec(memory_space=pltpu.SMEM)
params = pltpu.CompilerParams(vmem_limit_bytes=63 * 1024 * 1024)
tight = pltpu.CompilerParams(vmem_limit_bytes=54528 * 1024)
roomy = pltpu.CompilerParams(vmem_limit_bytes=24 * 1024 * 1024)


def after(value, other):
    return lax.optimization_barrier((value, other))[0]


def on_device(
    tokens,
    w_in,
    w_out,
    cache_keys,
    cache_values,
    session_slot,
    request_session,
    cand_count,
    hist_len,
):
    replicas = lax.axis_size("replica")
    groups = lax.axis_size("tensor")
    my_index = lax.axis_index("replica").astype(jnp.int32).reshape(1)
    group_index = lax.axis_index("tensor").astype(jnp.int32).reshape(1)
    rows, model_width = tokens.shape
    head_dim = w_in.shape[2] // 4
    requests = request_session.shape[0]
    cands = rows // requests
    history = cache_keys.shape[1]
    capacity = max(2, (2 * requests + replicas - 1) // replicas)
    slot_rows = replicas * capacity * cands
    w_flat = w_in.reshape(model_width, 4 * head_dim)
    slots = session_slot.reshape(1, -1)
    lengths = hist_len.reshape(1, -1)
    named = request_session.reshape(1, -1)
    counts = cand_count.reshape(1, -1)
    chunks = 4

    sent, info = pl.pallas_call(
        functools.partial(send_kernel, capacity, cands, chunks),
        in_specs=[HBM, HBM, VMEM, VMEM, VMEM, SMEM],
        out_specs=[HBM, HBM],
        out_shape=[jax.ShapeDtypeStruct((slot_rows, head_dim), bf16), jax.ShapeDtypeStruct((8, 128), f32)],
        scratch_shapes=[
            pltpu.VMEM((rows, model_width), bf16),
            pltpu.VMEM((model_width, head_dim), bf16),
            pltpu.VMEM((rows, head_dim), bf16),
            pltpu.VMEM((slot_rows, head_dim), bf16),
            pltpu.VMEM((8, 128), f32),
            pltpu.SemaphoreType.DMA((chunks,)),
            pltpu.SemaphoreType.DMA,
            pltpu.SemaphoreType.DMA((chunks + 1,)),
        ],
        compiler_params=params,
        name="send",
    )(tokens, w_flat, slots, named, lengths, my_index)
    got = lax.all_to_all(
        sent.reshape(replicas, capacity * cands, head_dim), "replica", split_axis=0, concat_axis=0, tiled=True
    )
    def passed(piece, by, flip=0):
        pairs = []
        for r in range(replicas):
            for z in range(groups):
                pairs.append((r * groups + z, (r ^ flip) * groups + (z + (by if r % 2 == 0 else -by)) % groups))
        return lax.ppermute(piece, ("replica", "tensor"), pairs)

    def swapped(piece):
        return lax.ppermute(piece, "replica", [(r, r ^ 1) for r in range(replicas)])

    w_own = after(w_out.reshape(head_dim, model_width), sent)
    next_one = passed(w_own, 1)
    next_two = passed(w_own, 2)
    mine = pl.pallas_call(
        functools.partial(local_kernel, capacity, cands),
        in_specs=[VMEM] * 6,
        out_specs=HBM,
        out_shape=jax.ShapeDtypeStruct((rows, 3 * head_dim), f32),
        scratch_shapes=[pltpu.VMEM((rows, 3 * head_dim), f32), pltpu.SemaphoreType.DMA],
        compiler_params=params,
        cost_estimate=pl.CostEstimate(flops=1 << 30, bytes_accessed=16 << 20, transcendentals=1 << 18),
        name="local",
    )(tokens, w_flat, slots, after(named, sent), counts, lengths)
    block = min(256, slot_rows)
    answers = pl.pallas_call(
        functools.partial(history_kernel, block),
        in_specs=[HBM, ANY, HBM, HBM],
        out_specs=HBM,
        out_shape=jax.ShapeDtypeStruct((slot_rows, head_dim), bf16),
        scratch_shapes=[
            pltpu.VMEM((8, 128), f32),
            pltpu.VMEM((slot_rows, head_dim), bf16),
            pltpu.VMEM((history, head_dim), bf16),
            pltpu.VMEM((history, head_dim), bf16),
            pltpu.VMEM((slot_rows, head_dim), bf16),
            pltpu.SemaphoreType.DMA((4 + slot_rows // block,)),
        ],
        compiler_params=tight,
        cost_estimate=pl.CostEstimate(flops=1 << 30, bytes_accessed=64 << 20, transcendentals=slot_rows * history),
        name="history",
    )(
        after(info, mine),
        got.reshape(slot_rows, head_dim),
        cache_keys.reshape(history, head_dim),
        cache_values.reshape(history, head_dim),
    )
    next_one, next_two = after((next_one, next_two), answers)
    nexts = jnp.concatenate([next_one, next_two], axis=0)
    lasts = passed(nexts, 2)
    others = swapped(nexts)
    other_three = passed(next_two, 1, flip=1)
    returned = lax.all_to_all(
        answers.reshape(replicas, capacity * cands, head_dim), "replica", split_axis=0, concat_axis=0, tiled=True
    )
    gated = pl.pallas_call(
        gate_kernel,
        in_specs=[ANY, HBM],
        out_specs=HBM,
        out_shape=jax.ShapeDtypeStruct((rows, head_dim), bf16),
        scratch_shapes=[
            pltpu.VMEM((slot_rows, head_dim), bf16),
            pltpu.VMEM((rows, 3 * head_dim), f32),
            pltpu.VMEM((rows, head_dim), bf16),
            pltpu.SemaphoreType.DMA((2,)),
        ],
        compiler_params=tight,
        cost_estimate=pl.CostEstimate(flops=1 << 30, bytes_accessed=64 << 20, transcendentals=1 << 10),
        name="gate",
    )(returned.reshape(slot_rows, head_dim), mine)
    share = rows // groups
    heads = lax.all_to_all(
        gated.reshape(groups, share, head_dim), "tensor", split_axis=0, concat_axis=0, tiled=True
    )
    return pl.pallas_call(
        output_kernel,
        in_specs=[SMEM, SMEM, HBM] + [ANY] * 6,
        out_specs=HBM,
        out_shape=jax.ShapeDtypeStruct((share, model_width), bf16),
        scratch_shapes=[
            pltpu.VMEM((groups, share, head_dim), bf16),
            pltpu.VMEM((groups * head_dim, model_width), bf16),
            pltpu.VMEM((share, model_width), bf16),
            pltpu.VMEM((share, model_width), bf16),
            pltpu.SemaphoreType.DMA((7,)),
        ],
        compiler_params=tight,
        name="output",
    )(group_index, my_index, tokens, heads, w_own, nexts, lasts, others, other_three)


def solution(mesh):
    in_specs = (
        P("replica", None),
        P(None, "tensor", None),
        P("tensor", None, None),
        P("replica", None, "tensor", None),
        P("replica", None, "tensor", None),
        P(),
        P("replica"),
        P("replica"),
        P(),
    )
    out_specs = P(("replica", "tensor"), None)
    return jax.shard_map(
        on_device, mesh=mesh, in_specs=in_specs, out_specs=out_specs, check_vma=False
    )
```

```python
import functools

import jax
import jax.numpy as jnp
from jax import lax
from jax.experimental import pallas as pl
from jax.experimental.pallas import tpu as pltpu
from jax.sharding import PartitionSpec as P

epsilon = 1e-05
f32 = jnp.float32
bf16 = jnp.bfloat16


def layer_norm(values):
    average = jnp.mean(values, -1, keepdims=True)
    centred = values - average
    return centred * lax.rsqrt(jnp.mean(centred * centred, -1, keepdims=True) + epsilon)


def silu(values):
    half = values * 0.5
    return half + half * jnp.tanh(half)


def iota(shape, dimension):
    return lax.broadcasted_iota(jnp.int32, shape, dimension)


def to_column(row):
    n = row.shape[1]
    return jnp.sum(jnp.where(iota((n, n), 0) == iota((n, n), 1), row, 0.0), 1, keepdims=True)


def lookup(table_row, index_row):
    sessions, requests = table_row.shape[1], index_row.shape[1]
    named = iota((sessions, requests), 0) == index_row
    return jnp.sum(jnp.where(named, to_column(table_row.astype(f32)), 0.0), 0, keepdims=True)


def first_rows(slot_ref, session_ref, capacity, cands):
    owner = lookup(slot_ref[...], session_ref[...])
    requests = owner.shape[1]
    square = (requests, requests)
    earlier = (to_column(owner) == owner) & (iota(square, 0) < iota(square, 1))
    rank = jnp.sum(jnp.where(earlier, 1.0, 0.0), 0, keepdims=True)
    return (owner * capacity + rank) * cands


def send_kernel(
    capacity, cands, chunks, tokens_ref, w_ref, slot_ref, session_ref, length_ref, me_ref, sent_ref, info_ref,
    held, weight, queries, placed, info, sems, w_sem, out_sems,
):
    rows = tokens_ref.shape[0]
    head_dim = weight.shape[1]
    slot_rows = sent_ref.shape[0]
    chunk = rows // chunks
    fetch_w = pltpu.make_async_copy(w_ref.at[:, pl.ds(2 * head_dim, head_dim)], weight, w_sem)
    fetches = [
        pltpu.make_async_copy(
            tokens_ref.at[pl.ds(n * chunk, chunk), :], held.at[pl.ds(n * chunk, chunk), :], sems.at[n]
        )
        for n in range(chunks)
    ]
    fetches[0].start()
    fetch_w.start()
    for fetch in fetches[1:]:
        fetch.start()
    for row, who in enumerate((me_ref[0], me_ref[0] ^ 1)):
        named = slot_ref[...] == who
        length = jnp.sum(jnp.where(named, length_ref[...].astype(f32), 0.0), 1, keepdims=True)
        info[row : row + 1, :] = jnp.broadcast_to(length, (1, info.shape[1]))
    core = (me_ref[0] & 1).astype(f32)
    info[2:, :] = jnp.broadcast_to(core, (info.shape[0] - 2, info.shape[1]))
    stores = [pltpu.make_async_copy(info, info_ref, out_sems.at[chunks])]
    stores[0].start()
    first = first_rows(slot_ref, session_ref, capacity, cands)
    requests = first.shape[1]
    spread = iota((requests, rows), 1) // cands == iota((requests, rows), 0)
    place = jnp.sum(jnp.where(spread, to_column(first), 0.0), 0, keepdims=True).astype(jnp.int32)
    place = place + iota((1, rows), 1) % cands
    for n, fetch in enumerate(fetches):
        part = pl.ds(n * chunk, chunk)
        fetch.wait()
        normed = layer_norm(held[part, :].astype(f32)).astype(bf16)
        if n == 0:
            fetch_w.wait()
        queries[part, :] = silu(jnp.dot(normed, weight[...], preferred_element_type=f32)).astype(bf16)
    block = slot_rows // chunks
    for n in range(chunks):
        part = pl.ds(n * block, block)
        chosen = jnp.where(iota((block, rows), 0) + n * block == place, 1.0, 0.0).astype(bf16)
        placed[part, :] = jnp.dot(chosen, queries[...], preferred_element_type=f32).astype(bf16)
        stores.append(pltpu.make_async_copy(placed.at[part, :], sent_ref.at[part, :], out_sems.at[n]))
        stores[-1].start()
    for store in stores:
        store.wait()


def local_kernel(
    capacity, cands, tokens_ref, w_ref, slot_ref, session_ref, count_ref, length_ref, out_ref, result, sem
):
    rows = tokens_ref.shape[0]
    head_dim = result.shape[1] // 3
    normed = layer_norm(tokens_ref[...].astype(f32)).astype(bf16)
    projected = silu(jnp.dot(normed, w_ref[...], preferred_element_type=f32)).astype(bf16).astype(f32)
    gate = projected[:, :head_dim]
    values = projected[:, head_dim : 2 * head_dim]
    queries = projected[:, 2 * head_dim : 3 * head_dim]
    keys = projected[:, 3 * head_dim :]
    lengths = lookup(length_ref[...], session_ref[...])
    requests = lengths.shape[1]
    spread = iota((rows, requests), 0) // cands == iota((rows, requests), 1)

    def per_row(row):
        return jnp.sum(jnp.where(spread, row, 0.0), 1, keepdims=True)

    within = (iota((rows, 1), 0) % cands).astype(f32)
    scores = jnp.sum(queries * keys, -1, keepdims=True) * head_dim ** (-0.5)
    result[:, :head_dim] = silu(scores) * values / (per_row(lengths) + 1.0)
    alive = within < per_row(count_ref[...].astype(f32))
    result[:, head_dim : 2 * head_dim] = jnp.where(alive, gate, 0.0)
    place = per_row(first_rows(slot_ref, session_ref, capacity, cands)) + within
    result[:, 2 * head_dim :] = jnp.broadcast_to(place, (rows, head_dim))
    store = pltpu.make_async_copy(result, out_ref, sem)
    store.start()
    store.wait()


def history_kernel(
    blocks, info_ref, query_ref, keys_ref, values_ref, other_keys_ref, other_values_ref, out_ref, result, sems
):
    history, head_dim = keys_ref.shape
    chips, _, held, _ = query_ref.shape
    share = chips // blocks
    half_scale = 0.5 * head_dim ** (-0.5)
    second = info_ref[2:3, :] > 0.5
    sides = []
    for row, keys, values in ((0, keys_ref, values_ref), (1, other_keys_ref, other_values_ref)):
        length = info_ref[row : row + 1, :1]
        seen = iota((history, 1), 0).astype(f32) < length
        sides.append((keys[...], jnp.where(seen, values[...], jnp.zeros((), bf16)), length + 1.0))
    stores = []
    for n in range(blocks):
        part = pl.ds(n * share, share)
        first_rows_of = query_ref[part, 0].reshape(share * held, head_dim)
        second_rows_of = query_ref[part, 1].reshape(share * held, head_dim)
        mine = jnp.where(second, second_rows_of, first_rows_of)
        others = jnp.where(second, first_rows_of, second_rows_of)
        answers = []
        for query, (keys, values, divisor) in zip((mine, others), sides):
            half = (
                lax.dot_general(query, keys, (((1,), (1,)), ((), ())), preferred_element_type=f32) * half_scale
            )
            weights = (half + half * jnp.tanh(half)).astype(bf16)
            summed = jnp.dot(weights, values, preferred_element_type=f32)
            answers.append((summed / divisor).astype(bf16))
        mine, others = answers
        result[part, 0] = jnp.where(second, others, mine).reshape(share, held, head_dim)
        result[part, 1] = jnp.where(second, mine, others).reshape(share, held, head_dim)
        stores.append(pltpu.make_async_copy(result.at[part], out_ref.at[part], sems.at[n]))
        stores[-1].start()
    for store in stores:
        store.wait()


def gate_kernel(returned_ref, mine_ref, out_ref, returned, mine, result, sems):
    fetches = [
        pltpu.make_async_copy(mine_ref, mine, sems.at[0]),
        pltpu.make_async_copy(returned_ref, returned, sems.at[1]),
    ]
    for fetch in fetches:
        fetch.start()
    rows, head_dim = result.shape
    slot_rows = returned.shape[0]
    fetches[0].wait()
    place = mine[:, 2 * head_dim : 2 * head_dim + 1].astype(jnp.int32)
    back = jnp.where(iota((rows, slot_rows), 1) == place, 1.0, 0.0).astype(bf16)
    fetches[1].wait()
    part = jnp.dot(back, returned[...], preferred_element_type=f32)
    result[...] = (layer_norm(part + mine[:, :head_dim]) * mine[:, head_dim : 2 * head_dim]).astype(bf16)
    store = pltpu.make_async_copy(result, out_ref, sems.at[0])
    store.start()
    store.wait()


held_heads = ((0, 1), (2, 3), (4, -1), (-2, -3))


def output_kernel(
    group_ref, me_ref, tokens_ref, gated_ref, own_ref, next_ref, last_ref, other_ref, three_ref,
    out_ref, gated, weight, tokens, result, sems,
):
    groups, share, head_dim = gated_ref.shape
    group = group_ref[0]
    sign = jnp.where(me_ref[0] % 2 == 0, -1, 1)
    double = 2 * head_dim
    fetches = [pltpu.make_async_copy(gated_ref, gated, sems.at[0])]
    start = 0
    for n, source in enumerate((own_ref, next_ref, last_ref, other_ref, three_ref)):
        size = source.shape[0]
        fetches.append(pltpu.make_async_copy(source, weight.at[pl.ds(start, size), :], sems.at[1 + n]))
        start += size
    mine = pl.ds(pl.multiple_of(group * share, share), share)
    fetch_tokens = pltpu.make_async_copy(tokens_ref.at[mine, :], tokens, sems.at[6])
    for fetch in fetches:
        fetch.start()
    fetch_tokens.start()
    total = jnp.zeros(result.shape, f32)
    for pair, waits in enumerate((fetches[:3], fetches[3:4], fetches[4:5], fetches[5:])):
        for fetch in waits:
            fetch.wait()
        rows = jnp.concatenate(
            [gated[lax.rem(group + sign * head + groups, groups)] for head in held_heads[pair]], axis=1
        )
        total = total + jnp.dot(rows, weight[pl.ds(pair * double, double), :], preferred_element_type=f32)
    fetch_tokens.wait()
    result[...] = (tokens[...].astype(f32) + total).astype(bf16)
    store = pltpu.make_async_copy(result, out_ref, sems.at[0])
    store.start()
    store.wait()


ANY = pl.BlockSpec(memory_space=pl.ANY)
HBM = pl.BlockSpec(memory_space=pltpu.HBM)
VMEM = pl.BlockSpec(memory_space=pltpu.VMEM)
SMEM = pl.BlockSpec(memory_space=pltpu.SMEM)
params = pltpu.CompilerParams(vmem_limit_bytes=63 * 1024 * 1024)
tight = pltpu.CompilerParams(vmem_limit_bytes=54528 * 1024)
roomy = pltpu.CompilerParams(vmem_limit_bytes=24 * 1024 * 1024)


def after(value, other):
    return lax.optimization_barrier((value, other))[0]


def on_device(
    tokens,
    w_in,
    w_out,
    cache_keys,
    cache_values,
    session_slot,
    request_session,
    cand_count,
    hist_len,
):
    replicas = lax.axis_size("replica")
    groups = lax.axis_size("tensor")
    my_index = lax.axis_index("replica").astype(jnp.int32).reshape(1)
    group_index = lax.axis_index("tensor").astype(jnp.int32).reshape(1)
    rows, model_width = tokens.shape
    head_dim = w_in.shape[2] // 4
    requests = request_session.shape[0]
    cands = rows // requests
    history = cache_keys.shape[1]
    capacity = max(2, (2 * requests + replicas - 1) // replicas)
    slot_rows = replicas * capacity * cands
    w_flat = w_in.reshape(model_width, 4 * head_dim)
    slots = session_slot.reshape(1, -1)
    lengths = hist_len.reshape(1, -1)
    named = request_session.reshape(1, -1)
    counts = cand_count.reshape(1, -1)
    chunks = 4

    sent, info = pl.pallas_call(
        functools.partial(send_kernel, capacity, cands, chunks),
        in_specs=[HBM, HBM, VMEM, VMEM, VMEM, SMEM],
        out_specs=[HBM, HBM],
        out_shape=[jax.ShapeDtypeStruct((slot_rows, head_dim), bf16), jax.ShapeDtypeStruct((8, 128), f32)],
        scratch_shapes=[
            pltpu.VMEM((rows, model_width), bf16),
            pltpu.VMEM((model_width, head_dim), bf16),
            pltpu.VMEM((rows, head_dim), bf16),
            pltpu.VMEM((slot_rows, head_dim), bf16),
            pltpu.VMEM((8, 128), f32),
            pltpu.SemaphoreType.DMA((chunks,)),
            pltpu.SemaphoreType.DMA,
            pltpu.SemaphoreType.DMA((chunks + 1,)),
        ],
        compiler_params=params,
        name="send",
    )(tokens, w_flat, slots, named, lengths, my_index)
    chips = replicas // 2
    held = capacity * cands
    same_core = [[2 * chip + core for chip in range(chips)] for core in range(2)]

    def exchanged(rows_of):
        return lax.all_to_all(
            rows_of.reshape(chips, 2 * held, head_dim),
            "replica",
            split_axis=0,
            concat_axis=0,
            tiled=True,
            axis_index_groups=same_core,
        )

    got = exchanged(sent)

    def passed(piece, by, flip=0):
        pairs = []
        for r in range(replicas):
            for z in range(groups):
                pairs.append((r * groups + z, (r ^ flip) * groups + (z + (by if r % 2 == 0 else -by)) % groups))
        return lax.ppermute(piece, ("replica", "tensor"), pairs)

    def swapped(piece):
        return lax.ppermute(piece, "replica", [(r, r ^ 1) for r in range(replicas)])

    w_own = after(w_out.reshape(head_dim, model_width), sent)
    next_one = passed(w_own, 1)
    next_two = passed(w_own, 2)
    mine = pl.pallas_call(
        functools.partial(local_kernel, capacity, cands),
        in_specs=[VMEM] * 6,
        out_specs=HBM,
        out_shape=jax.ShapeDtypeStruct((rows, 3 * head_dim), f32),
        scratch_shapes=[pltpu.VMEM((rows, 3 * head_dim), f32), pltpu.SemaphoreType.DMA],
        compiler_params=roomy,
        cost_estimate=pl.CostEstimate(flops=1 << 30, bytes_accessed=16 << 20, transcendentals=1 << 18),
        name="local",
    )(tokens, w_flat, slots, after(named, sent), counts, lengths)
    keys = cache_keys.reshape(history, head_dim)
    values = cache_values.reshape(history, head_dim)
    other_keys, other_values = swapped(after(keys, sent)), swapped(after(values, sent))
    blocks = 2
    answers = pl.pallas_call(
        functools.partial(history_kernel, blocks),
        in_specs=[VMEM] * 6,
        out_specs=HBM,
        out_shape=jax.ShapeDtypeStruct((chips, 2, held, head_dim), bf16),
        scratch_shapes=[
            pltpu.VMEM((chips, 2, held, head_dim), bf16),
            pltpu.SemaphoreType.DMA((blocks,)),
        ],
        compiler_params=roomy,
        cost_estimate=pl.CostEstimate(flops=1 << 30, bytes_accessed=64 << 20, transcendentals=slot_rows * history),
        name="history",
    )(
        after(info, mine),
        got.reshape(chips, 2, held, head_dim),
        keys,
        values,
        other_keys,
        other_values,
    )
    next_one, next_two = after((next_one, next_two), answers)
    nexts = jnp.concatenate([next_one, next_two], axis=0)
    lasts = passed(nexts, 2)
    others = swapped(nexts)
    other_three = passed(next_two, 1, flip=1)
    returned = exchanged(answers)
    gated = pl.pallas_call(
        gate_kernel,
        in_specs=[ANY, HBM],
        out_specs=HBM,
        out_shape=jax.ShapeDtypeStruct((rows, head_dim), bf16),
        scratch_shapes=[
            pltpu.VMEM((slot_rows, head_dim), bf16),
            pltpu.VMEM((rows, 3 * head_dim), f32),
            pltpu.VMEM((rows, head_dim), bf16),
            pltpu.SemaphoreType.DMA((2,)),
        ],
        compiler_params=tight,
        cost_estimate=pl.CostEstimate(flops=1 << 30, bytes_accessed=64 << 20, transcendentals=1 << 10),
        name="gate",
    )(returned.reshape(slot_rows, head_dim), mine)
    share = rows // groups
    heads = lax.all_to_all(
        gated.reshape(groups, share, head_dim), "tensor", split_axis=0, concat_axis=0, tiled=True
    )
    return pl.pallas_call(
        output_kernel,
        in_specs=[SMEM, SMEM, HBM] + [ANY] * 6,
        out_specs=HBM,
        out_shape=jax.ShapeDtypeStruct((share, model_width), bf16),
        scratch_shapes=[
            pltpu.VMEM((groups, share, head_dim), bf16),
            pltpu.VMEM((groups * head_dim, model_width), bf16),
            pltpu.VMEM((share, model_width), bf16),
            pltpu.VMEM((share, model_width), bf16),
            pltpu.SemaphoreType.DMA((7,)),
        ],
        compiler_params=tight,
        name="output",
    )(group_index, my_index, tokens, heads, w_own, nexts, lasts, others, other_three)


def solution(mesh):
    in_specs = (
        P("replica", None),
        P(None, "tensor", None),
        P("tensor", None, None),
        P("replica", None, "tensor", None),
        P("replica", None, "tensor", None),
        P(),
        P("replica"),
        P("replica"),
        P(),
    )
    out_specs = P(("replica", "tensor"), None)
    return jax.shard_map(
        on_device, mesh=mesh, in_specs=in_specs, out_specs=out_specs, check_vma=False
    )
```

```python
import functools

import jax
import jax.numpy as jnp
from jax import lax
from jax.experimental import pallas as pl
from jax.experimental.pallas import tpu as pltpu
from jax.sharding import PartitionSpec as P

epsilon = 1e-05
f32 = jnp.float32
bf16 = jnp.bfloat16


def layer_norm(values):
    average = jnp.mean(values, -1, keepdims=True)
    centred = values - average
    return centred * lax.rsqrt(jnp.mean(centred * centred, -1, keepdims=True) + epsilon)


def silu(values):
    half = values * 0.5
    return half + half * jnp.tanh(half)


def iota(shape, dimension):
    return lax.broadcasted_iota(jnp.int32, shape, dimension)


def to_column(row):
    n = row.shape[1]
    return jnp.sum(jnp.where(iota((n, n), 0) == iota((n, n), 1), row, 0.0), 1, keepdims=True)


def lookup(table_row, index_row):
    sessions, requests = table_row.shape[1], index_row.shape[1]
    named = iota((sessions, requests), 0) == index_row
    return jnp.sum(jnp.where(named, to_column(table_row.astype(f32)), 0.0), 0, keepdims=True)


def first_rows(slot_ref, session_ref, capacity, cands):
    owner = lookup(slot_ref[...], session_ref[...])
    requests = owner.shape[1]
    square = (requests, requests)
    earlier = (to_column(owner) == owner) & (iota(square, 0) < iota(square, 1))
    rank = jnp.sum(jnp.where(earlier, 1.0, 0.0), 0, keepdims=True)
    return (owner * capacity + rank) * cands


def send_kernel(
    capacity, cands, chunks, tokens_ref, w_ref, slot_ref, session_ref, length_ref, me_ref, sent_ref, info_ref,
    held, weight, queries, placed, info, sems, w_sem, out_sems,
):
    rows = tokens_ref.shape[0]
    head_dim = weight.shape[1]
    slot_rows = sent_ref.shape[0]
    chunk = rows // chunks
    fetch_w = pltpu.make_async_copy(w_ref.at[:, pl.ds(2 * head_dim, head_dim)], weight, w_sem)
    fetches = [
        pltpu.make_async_copy(
            tokens_ref.at[pl.ds(n * chunk, chunk), :], held.at[pl.ds(n * chunk, chunk), :], sems.at[n]
        )
        for n in range(chunks)
    ]
    fetches[0].start()
    fetch_w.start()
    for fetch in fetches[1:]:
        fetch.start()
    own = slot_ref[...] == me_ref[0]
    length = jnp.sum(jnp.where(own, length_ref[...].astype(f32), 0.0), 1, keepdims=True)
    info[...] = jnp.broadcast_to(length, info.shape)
    stores = [pltpu.make_async_copy(info, info_ref, out_sems.at[chunks])]
    stores[0].start()
    first = first_rows(slot_ref, session_ref, capacity, cands)
    requests = first.shape[1]
    spread = iota((requests, rows), 1) // cands == iota((requests, rows), 0)
    place = jnp.sum(jnp.where(spread, to_column(first), 0.0), 0, keepdims=True).astype(jnp.int32)
    place = place + iota((1, rows), 1) % cands
    for n, fetch in enumerate(fetches):
        part = pl.ds(n * chunk, chunk)
        fetch.wait()
        normed = layer_norm(held[part, :].astype(f32)).astype(bf16)
        if n == 0:
            fetch_w.wait()
        queries[part, :] = silu(jnp.dot(normed, weight[...], preferred_element_type=f32)).astype(bf16)
    block = slot_rows // chunks
    for n in range(chunks):
        part = pl.ds(n * block, block)
        chosen = jnp.where(iota((block, rows), 0) + n * block == place, 1.0, 0.0).astype(bf16)
        placed[part, :] = jnp.dot(chosen, queries[...], preferred_element_type=f32).astype(bf16)
        stores.append(pltpu.make_async_copy(placed.at[part, :], sent_ref.at[part, :], out_sems.at[n]))
        stores[-1].start()
    for store in stores:
        store.wait()


def local_kernel(
    capacity, cands, tokens_ref, w_ref, slot_ref, session_ref, count_ref, length_ref, result
):
    rows = tokens_ref.shape[0]
    head_dim = result.shape[1] // 3
    normed = layer_norm(tokens_ref[...].astype(f32)).astype(bf16)
    projected = silu(jnp.dot(normed, w_ref[...], preferred_element_type=f32)).astype(bf16).astype(f32)
    gate = projected[:, :head_dim]
    values = projected[:, head_dim : 2 * head_dim]
    queries = projected[:, 2 * head_dim : 3 * head_dim]
    keys = projected[:, 3 * head_dim :]
    lengths = lookup(length_ref[...], session_ref[...])
    requests = lengths.shape[1]
    spread = iota((rows, requests), 0) // cands == iota((rows, requests), 1)

    def per_row(row):
        return jnp.sum(jnp.where(spread, row, 0.0), 1, keepdims=True)

    within = (iota((rows, 1), 0) % cands).astype(f32)
    scores = jnp.sum(queries * keys, -1, keepdims=True) * head_dim ** (-0.5)
    result[:, :head_dim] = silu(scores) * values / (per_row(lengths) + 1.0)
    alive = within < per_row(count_ref[...].astype(f32))
    result[:, head_dim : 2 * head_dim] = jnp.where(alive, gate, 0.0)
    place = per_row(first_rows(slot_ref, session_ref, capacity, cands)) + within
    result[:, 2 * head_dim :] = jnp.broadcast_to(place, (rows, head_dim))


def history_kernel(block, info_ref, query_ref, keys_ref, values_ref, out_ref, result, sems):
    history, head_dim = keys_ref.shape
    half_scale = 0.5 * head_dim ** (-0.5)
    length = info_ref[:1, :1]
    divisor = length + 1.0
    seen = iota((history, 1), 0).astype(f32) < length
    seen_values = jnp.where(seen, values_ref[...], jnp.zeros((), bf16))
    stores = []
    for n, start in enumerate(range(0, query_ref.shape[0], block)):
        part = pl.ds(start, block)
        half = (
            lax.dot_general(
                query_ref[part, :], keys_ref[...], (((1,), (1,)), ((), ())), preferred_element_type=f32
            )
            * half_scale
        )
        weights = (half + half * jnp.tanh(half)).astype(bf16)
        summed = jnp.dot(weights, seen_values, preferred_element_type=f32)
        result[part, :] = (summed / divisor).astype(bf16)
        stores.append(pltpu.make_async_copy(result.at[part, :], out_ref.at[part, :], sems.at[n]))
        stores[-1].start()
    for store in stores:
        store.wait()


def gate_kernel(returned_ref, mine_ref, out_ref, returned, mine, result, sems):
    fetches = [
        pltpu.make_async_copy(mine_ref, mine, sems.at[0]),
        pltpu.make_async_copy(returned_ref, returned, sems.at[1]),
    ]
    for fetch in fetches:
        fetch.start()
    rows, head_dim = result.shape
    slot_rows = returned.shape[0]
    fetches[0].wait()
    place = mine[:, 2 * head_dim : 2 * head_dim + 1].astype(jnp.int32)
    back = jnp.where(iota((rows, slot_rows), 1) == place, 1.0, 0.0).astype(bf16)
    fetches[1].wait()
    part = jnp.dot(back, returned[...], preferred_element_type=f32)
    result[...] = (layer_norm(part + mine[:, :head_dim]) * mine[:, head_dim : 2 * head_dim]).astype(bf16)
    store = pltpu.make_async_copy(result, out_ref, sems.at[0])
    store.start()
    store.wait()


def output_kernel(
    group_ref, me_ref, tokens_ref, gated_ref, own_ref, next_ref, last_ref, other_ref, three_ref,
    out_ref, tokens, result, sems,
):
    groups, share, head_dim = gated_ref.shape
    group = group_ref[0]
    mine = pl.ds(pl.multiple_of(group * share, share), share)
    fetch_tokens = pltpu.make_async_copy(tokens_ref.at[mine, :], tokens, sems.at[0])
    fetch_tokens.start()
    sign = jnp.where(me_ref[0] % 2 == 0, -1, 1)
    total = jnp.zeros(result.shape, f32)
    for heads, weight in (
        ((1, 2), next_ref[...]),
        ((3, 4), last_ref[...]),
        ((-1, -2), other_ref[...]),
        ((0, -3), jnp.concatenate([own_ref[...], three_ref[...]], axis=0)),
    ):
        rows = jnp.concatenate([gated_ref[lax.rem(group + sign * head + groups, groups)] for head in heads], axis=1)
        total = total + jnp.dot(rows, weight, preferred_element_type=f32)
    fetch_tokens.wait()
    result[...] = (tokens[...].astype(f32) + total).astype(bf16)
    store = pltpu.make_async_copy(result, out_ref, sems.at[1])
    store.start()
    store.wait()


ANY = pl.BlockSpec(memory_space=pl.ANY)
HBM = pl.BlockSpec(memory_space=pltpu.HBM)
VMEM = pl.BlockSpec(memory_space=pltpu.VMEM)
SMEM = pl.BlockSpec(memory_space=pltpu.SMEM)
params = pltpu.CompilerParams(vmem_limit_bytes=63 * 1024 * 1024)
tight = pltpu.CompilerParams(vmem_limit_bytes=54528 * 1024)
roomy = pltpu.CompilerParams(vmem_limit_bytes=24 * 1024 * 1024)


def after(value, other):
    return lax.optimization_barrier((value, other))[0]


def on_device(
    tokens,
    w_in,
    w_out,
    cache_keys,
    cache_values,
    session_slot,
    request_session,
    cand_count,
    hist_len,
):
    replicas = lax.axis_size("replica")
    groups = lax.axis_size("tensor")
    my_index = lax.axis_index("replica").astype(jnp.int32).reshape(1)
    group_index = lax.axis_index("tensor").astype(jnp.int32).reshape(1)
    rows, model_width = tokens.shape
    head_dim = w_in.shape[2] // 4
    requests = request_session.shape[0]
    cands = rows // requests
    history = cache_keys.shape[1]
    capacity = max(2, (2 * requests + replicas - 1) // replicas)
    slot_rows = replicas * capacity * cands
    w_flat = w_in.reshape(model_width, 4 * head_dim)
    slots = session_slot.reshape(1, -1)
    lengths = hist_len.reshape(1, -1)
    named = request_session.reshape(1, -1)
    counts = cand_count.reshape(1, -1)
    chunks = 4

    sent, info = pl.pallas_call(
        functools.partial(send_kernel, capacity, cands, chunks),
        in_specs=[HBM, HBM, VMEM, VMEM, VMEM, SMEM],
        out_specs=[HBM, HBM],
        out_shape=[jax.ShapeDtypeStruct((slot_rows, head_dim), bf16), jax.ShapeDtypeStruct((8, 128), f32)],
        scratch_shapes=[
            pltpu.VMEM((rows, model_width), bf16),
            pltpu.VMEM((model_width, head_dim), bf16),
            pltpu.VMEM((rows, head_dim), bf16),
            pltpu.VMEM((slot_rows, head_dim), bf16),
            pltpu.VMEM((8, 128), f32),
            pltpu.SemaphoreType.DMA((chunks,)),
            pltpu.SemaphoreType.DMA,
            pltpu.SemaphoreType.DMA((chunks + 1,)),
        ],
        compiler_params=params,
        name="send",
    )(tokens, w_flat, slots, named, lengths, my_index)
    got = lax.all_to_all(
        sent.reshape(replicas, capacity * cands, head_dim), "replica", split_axis=0, concat_axis=0, tiled=True
    )
    def passed(piece, by, flip=0):
        pairs = []
        for r in range(replicas):
            for z in range(groups):
                pairs.append((r * groups + z, (r ^ flip) * groups + (z + (by if r % 2 == 0 else -by)) % groups))
        return lax.ppermute(piece, ("replica", "tensor"), pairs)

    def swapped(piece):
        return lax.ppermute(piece, "replica", [(r, r ^ 1) for r in range(replicas)])

    w_own = after(w_out.reshape(head_dim, model_width), sent)
    next_one = passed(w_own, 1)
    next_two = passed(w_own, 2)
    mine = pl.pallas_call(
        functools.partial(local_kernel, capacity, cands),
        in_specs=[VMEM] * 6,
        out_specs=VMEM,
        out_shape=jax.ShapeDtypeStruct((rows, 3 * head_dim), f32),
        compiler_params=roomy,
        cost_estimate=pl.CostEstimate(flops=1 << 30, bytes_accessed=16 << 20, transcendentals=1 << 18),
        name="local",
    )(tokens, w_flat, slots, after(named, sent), counts, lengths)
    block = min(256, slot_rows)
    answers = pl.pallas_call(
        functools.partial(history_kernel, block),
        in_specs=[VMEM] * 4,
        out_specs=HBM,
        out_shape=jax.ShapeDtypeStruct((slot_rows, head_dim), bf16),
        scratch_shapes=[
            pltpu.VMEM((slot_rows, head_dim), bf16),
            pltpu.SemaphoreType.DMA((slot_rows // block,)),
        ],
        compiler_params=roomy,
        cost_estimate=pl.CostEstimate(flops=1 << 30, bytes_accessed=64 << 20, transcendentals=slot_rows * history),
        name="history",
    )(
        after(info, mine),
        got.reshape(slot_rows, head_dim),
        cache_keys.reshape(history, head_dim),
        cache_values.reshape(history, head_dim),
    )
    next_one, next_two = after((next_one, next_two), answers)
    nexts = jnp.concatenate([next_one, next_two], axis=0)
    lasts = passed(nexts, 2)
    others = swapped(nexts)
    other_three = passed(next_two, 1, flip=1)
    returned = lax.all_to_all(
        answers.reshape(replicas, capacity * cands, head_dim), "replica", split_axis=0, concat_axis=0, tiled=True
    )
    gated = pl.pallas_call(
        gate_kernel,
        in_specs=[ANY, HBM],
        out_specs=HBM,
        out_shape=jax.ShapeDtypeStruct((rows, head_dim), bf16),
        scratch_shapes=[
            pltpu.VMEM((slot_rows, head_dim), bf16),
            pltpu.VMEM((rows, 3 * head_dim), f32),
            pltpu.VMEM((rows, head_dim), bf16),
            pltpu.SemaphoreType.DMA((2,)),
        ],
        compiler_params=tight,
        cost_estimate=pl.CostEstimate(flops=1 << 30, bytes_accessed=64 << 20, transcendentals=1 << 10),
        name="gate",
    )(returned.reshape(slot_rows, head_dim), mine)
    share = rows // groups
    heads = lax.all_to_all(
        gated.reshape(groups, share, head_dim), "tensor", split_axis=0, concat_axis=0, tiled=True
    )
    return pl.pallas_call(
        output_kernel,
        in_specs=[SMEM, SMEM, HBM] + [VMEM] * 6,
        out_specs=HBM,
        out_shape=jax.ShapeDtypeStruct((share, model_width), bf16),
        scratch_shapes=[
            pltpu.VMEM((share, model_width), bf16),
            pltpu.VMEM((share, model_width), bf16),
            pltpu.SemaphoreType.DMA((2,)),
        ],
        compiler_params=roomy,
        name="output",
    )(group_index, my_index, tokens, heads, w_own, nexts, lasts, others, other_three)


def solution(mesh):
    in_specs = (
        P("replica", None),
        P(None, "tensor", None),
        P("tensor", None, None),
        P("replica", None, "tensor", None),
        P("replica", None, "tensor", None),
        P(),
        P("replica"),
        P("replica"),
        P(),
    )
    out_specs = P(("replica", "tensor"), None)
    return jax.shard_map(
        on_device, mesh=mesh, in_specs=in_specs, out_specs=out_specs, check_vma=False
    )
```

```python
import functools

import jax
import jax.numpy as jnp
from jax import lax
from jax.experimental import pallas as pl
from jax.experimental.pallas import tpu as pltpu
from jax.sharding import PartitionSpec as P

epsilon = 1e-05
f32 = jnp.float32
bf16 = jnp.bfloat16


def layer_norm(values):
    average = jnp.mean(values, -1, keepdims=True)
    centred = values - average
    return centred * lax.rsqrt(jnp.mean(centred * centred, -1, keepdims=True) + epsilon)


def silu(values):
    half = values * 0.5
    return half + half * jnp.tanh(half)


def iota(shape, dimension):
    return lax.broadcasted_iota(jnp.int32, shape, dimension)


def to_column(row):
    n = row.shape[1]
    return jnp.sum(jnp.where(iota((n, n), 0) == iota((n, n), 1), row, 0.0), 1, keepdims=True)


def lookup(table_row, index_row):
    sessions, requests = table_row.shape[1], index_row.shape[1]
    named = iota((sessions, requests), 0) == index_row
    return jnp.sum(jnp.where(named, to_column(table_row.astype(f32)), 0.0), 0, keepdims=True)


def first_rows(slot_ref, session_ref, capacity, cands):
    owner = lookup(slot_ref[...], session_ref[...])
    requests = owner.shape[1]
    square = (requests, requests)
    earlier = (to_column(owner) == owner) & (iota(square, 0) < iota(square, 1))
    rank = jnp.sum(jnp.where(earlier, 1.0, 0.0), 0, keepdims=True)
    return (owner * capacity + rank) * cands


def send_kernel(
    capacity, cands, chunks, tokens_ref, w_ref, slot_ref, session_ref, length_ref, me_ref, sent_ref, info_ref,
    held, weight, queries, placed, info, sems, w_sem, out_sems,
):
    rows = tokens_ref.shape[0]
    head_dim = weight.shape[1]
    slot_rows = sent_ref.shape[0]
    chunk = rows // chunks
    fetch_w = pltpu.make_async_copy(w_ref.at[:, pl.ds(2 * head_dim, head_dim)], weight, w_sem)
    fetches = [
        pltpu.make_async_copy(
            tokens_ref.at[pl.ds(n * chunk, chunk), :], held.at[pl.ds(n * chunk, chunk), :], sems.at[n]
        )
        for n in range(chunks)
    ]
    fetches[0].start()
    fetch_w.start()
    for fetch in fetches[1:]:
        fetch.start()
    own = slot_ref[...] == me_ref[0]
    length = jnp.sum(jnp.where(own, length_ref[...].astype(f32), 0.0), 1, keepdims=True)
    info[...] = jnp.broadcast_to(length, info.shape)
    stores = [pltpu.make_async_copy(info, info_ref, out_sems.at[chunks])]
    stores[0].start()
    first = first_rows(slot_ref, session_ref, capacity, cands)
    requests = first.shape[1]
    spread = iota((requests, rows), 1) // cands == iota((requests, rows), 0)
    place = jnp.sum(jnp.where(spread, to_column(first), 0.0), 0, keepdims=True).astype(jnp.int32)
    place = place + iota((1, rows), 1) % cands
    for n, fetch in enumerate(fetches):
        part = pl.ds(n * chunk, chunk)
        fetch.wait()
        normed = layer_norm(held[part, :].astype(f32)).astype(bf16)
        if n == 0:
            fetch_w.wait()
        queries[part, :] = silu(jnp.dot(normed, weight[...], preferred_element_type=f32)).astype(bf16)
    block = slot_rows // chunks
    for n in range(chunks):
        part = pl.ds(n * block, block)
        chosen = jnp.where(iota((block, rows), 0) + n * block == place, 1.0, 0.0).astype(bf16)
        placed[part, :] = jnp.dot(chosen, queries[...], preferred_element_type=f32).astype(bf16)
        stores.append(pltpu.make_async_copy(placed.at[part, :], sent_ref.at[part, :], out_sems.at[n]))
        stores[-1].start()
    for store in stores:
        store.wait()


def local_kernel(
    capacity, cands, tokens_ref, w_ref, slot_ref, session_ref, count_ref, length_ref, result
):
    rows = tokens_ref.shape[0]
    head_dim = result.shape[1] // 3
    normed = layer_norm(tokens_ref[...].astype(f32)).astype(bf16)
    projected = silu(jnp.dot(normed, w_ref[...], preferred_element_type=f32)).astype(bf16).astype(f32)
    gate = projected[:, :head_dim]
    values = projected[:, head_dim : 2 * head_dim]
    queries = projected[:, 2 * head_dim : 3 * head_dim]
    keys = projected[:, 3 * head_dim :]
    lengths = lookup(length_ref[...], session_ref[...])
    requests = lengths.shape[1]
    spread = iota((rows, requests), 0) // cands == iota((rows, requests), 1)

    def per_row(row):
        return jnp.sum(jnp.where(spread, row, 0.0), 1, keepdims=True)

    within = (iota((rows, 1), 0) % cands).astype(f32)
    scores = jnp.sum(queries * keys, -1, keepdims=True) * head_dim ** (-0.5)
    result[:, :head_dim] = silu(scores) * values / (per_row(lengths) + 1.0)
    alive = within < per_row(count_ref[...].astype(f32))
    result[:, head_dim : 2 * head_dim] = jnp.where(alive, gate, 0.0)
    place = per_row(first_rows(slot_ref, session_ref, capacity, cands)) + within
    result[:, 2 * head_dim :] = jnp.broadcast_to(place, (rows, head_dim))


def history_kernel(block, info_ref, query_ref, keys_ref, values_ref, out_ref, result, sems):
    history, head_dim = keys_ref.shape
    half_scale = 0.5 * head_dim ** (-0.5)
    length = info_ref[:1, :1]
    divisor = length + 1.0
    seen = iota((history, 1), 0).astype(f32) < length
    seen_values = jnp.where(seen, values_ref[...], jnp.zeros((), bf16))
    stores = []
    for n, start in enumerate(range(0, query_ref.shape[0], block)):
        part = pl.ds(start, block)
        half = (
            lax.dot_general(
                query_ref[part, :], keys_ref[...], (((1,), (1,)), ((), ())), preferred_element_type=f32
            )
            * half_scale
        )
        weights = (half + half * jnp.tanh(half)).astype(bf16)
        summed = jnp.dot(weights, seen_values, preferred_element_type=f32)
        result[part, :] = (summed / divisor).astype(bf16)
        stores.append(pltpu.make_async_copy(result.at[part, :], out_ref.at[part, :], sems.at[n]))
        stores[-1].start()
    for store in stores:
        store.wait()


def gate_kernel(returned_ref, mine_ref, out_ref, returned, mine, result, sems):
    fetches = [
        pltpu.make_async_copy(mine_ref, mine, sems.at[0]),
        pltpu.make_async_copy(returned_ref, returned, sems.at[1]),
    ]
    for fetch in fetches:
        fetch.start()
    rows, head_dim = result.shape
    slot_rows = returned.shape[0]
    fetches[0].wait()
    place = mine[:, 2 * head_dim : 2 * head_dim + 1].astype(jnp.int32)
    back = jnp.where(iota((rows, slot_rows), 1) == place, 1.0, 0.0).astype(bf16)
    fetches[1].wait()
    part = jnp.dot(back, returned[...], preferred_element_type=f32)
    result[...] = (layer_norm(part + mine[:, :head_dim]) * mine[:, head_dim : 2 * head_dim]).astype(bf16)
    store = pltpu.make_async_copy(result, out_ref, sems.at[0])
    store.start()
    store.wait()


def output_kernel(
    group_ref, me_ref, tokens_ref, gated_ref, own_ref, next_ref, last_ref, other_ref, two_ref,
    out_ref, tokens, result, sems,
):
    groups, share, head_dim = gated_ref.shape
    group = group_ref[0]
    mine = pl.ds(pl.multiple_of(group * share, share), share)
    fetch_tokens = pltpu.make_async_copy(tokens_ref.at[mine, :], tokens, sems.at[0])
    fetch_tokens.start()
    sign = jnp.where(me_ref[0] % 2 == 0, -1, 1)
    total = jnp.zeros(result.shape, f32)
    for heads, weight in (
        ((1, 3), next_ref[...]),
        ((2, 4), last_ref[...]),
        ((-1, -3), other_ref[...]),
        ((0, -2), jnp.concatenate([own_ref[...], two_ref[...]], axis=0)),
    ):
        rows = jnp.concatenate([gated_ref[lax.rem(group + sign * head + groups, groups)] for head in heads], axis=1)
        total = total + jnp.dot(rows, weight, preferred_element_type=f32)
    fetch_tokens.wait()
    result[...] = (tokens[...].astype(f32) + total).astype(bf16)
    store = pltpu.make_async_copy(result, out_ref, sems.at[1])
    store.start()
    store.wait()


ANY = pl.BlockSpec(memory_space=pl.ANY)
HBM = pl.BlockSpec(memory_space=pltpu.HBM)
VMEM = pl.BlockSpec(memory_space=pltpu.VMEM)
SMEM = pl.BlockSpec(memory_space=pltpu.SMEM)
params = pltpu.CompilerParams(vmem_limit_bytes=63 * 1024 * 1024)
tight = pltpu.CompilerParams(vmem_limit_bytes=54528 * 1024)
roomy = pltpu.CompilerParams(vmem_limit_bytes=24 * 1024 * 1024)


def after(value, other):
    return lax.optimization_barrier((value, other))[0]


def on_device(
    tokens,
    w_in,
    w_out,
    cache_keys,
    cache_values,
    session_slot,
    request_session,
    cand_count,
    hist_len,
):
    replicas = lax.axis_size("replica")
    groups = lax.axis_size("tensor")
    my_index = lax.axis_index("replica").astype(jnp.int32).reshape(1)
    group_index = lax.axis_index("tensor").astype(jnp.int32).reshape(1)
    rows, model_width = tokens.shape
    head_dim = w_in.shape[2] // 4
    requests = request_session.shape[0]
    cands = rows // requests
    history = cache_keys.shape[1]
    capacity = max(2, (2 * requests + replicas - 1) // replicas)
    slot_rows = replicas * capacity * cands
    w_flat = w_in.reshape(model_width, 4 * head_dim)
    slots = session_slot.reshape(1, -1)
    lengths = hist_len.reshape(1, -1)
    named = request_session.reshape(1, -1)
    counts = cand_count.reshape(1, -1)
    chunks = 4

    sent, info = pl.pallas_call(
        functools.partial(send_kernel, capacity, cands, chunks),
        in_specs=[HBM, HBM, VMEM, VMEM, VMEM, SMEM],
        out_specs=[HBM, HBM],
        out_shape=[jax.ShapeDtypeStruct((slot_rows, head_dim), bf16), jax.ShapeDtypeStruct((8, 128), f32)],
        scratch_shapes=[
            pltpu.VMEM((rows, model_width), bf16),
            pltpu.VMEM((model_width, head_dim), bf16),
            pltpu.VMEM((rows, head_dim), bf16),
            pltpu.VMEM((slot_rows, head_dim), bf16),
            pltpu.VMEM((8, 128), f32),
            pltpu.SemaphoreType.DMA((chunks,)),
            pltpu.SemaphoreType.DMA,
            pltpu.SemaphoreType.DMA((chunks + 1,)),
        ],
        compiler_params=params,
        name="send",
    )(tokens, w_flat, slots, named, lengths, my_index)
    got = lax.all_to_all(
        sent.reshape(replicas, capacity * cands, head_dim), "replica", split_axis=0, concat_axis=0, tiled=True
    )
    def passed(piece, by, flip=0):
        pairs = []
        for r in range(replicas):
            for z in range(groups):
                pairs.append((r * groups + z, (r ^ flip) * groups + (z + (by if r % 2 == 0 else -by)) % groups))
        return lax.ppermute(piece, ("replica", "tensor"), pairs)

    def swapped(piece):
        return lax.ppermute(piece, "replica", [(r, r ^ 1) for r in range(replicas)])

    w_own = after(w_out.reshape(head_dim, model_width), sent)
    next_one = passed(w_own, 1)
    next_three = passed(w_own, 3)
    mine = pl.pallas_call(
        functools.partial(local_kernel, capacity, cands),
        in_specs=[VMEM] * 6,
        out_specs=VMEM,
        out_shape=jax.ShapeDtypeStruct((rows, 3 * head_dim), f32),
        compiler_params=roomy,
        cost_estimate=pl.CostEstimate(flops=1 << 30, bytes_accessed=16 << 20, transcendentals=1 << 18),
        name="local",
    )(tokens, w_flat, slots, after(named, sent), counts, lengths)
    block = min(256, slot_rows)
    answers = pl.pallas_call(
        functools.partial(history_kernel, block),
        in_specs=[VMEM] * 4,
        out_specs=HBM,
        out_shape=jax.ShapeDtypeStruct((slot_rows, head_dim), bf16),
        scratch_shapes=[
            pltpu.VMEM((slot_rows, head_dim), bf16),
            pltpu.SemaphoreType.DMA((slot_rows // block,)),
        ],
        compiler_params=roomy,
        cost_estimate=pl.CostEstimate(flops=1 << 30, bytes_accessed=64 << 20, transcendentals=slot_rows * history),
        name="history",
    )(
        after(info, mine),
        got.reshape(slot_rows, head_dim),
        cache_keys.reshape(history, head_dim),
        cache_values.reshape(history, head_dim),
    )
    next_one, next_three = after((next_one, next_three), answers)
    nexts = jnp.concatenate([next_one, next_three], axis=0)
    lasts = passed(nexts, 1)
    others = swapped(nexts)
    other_two = passed(next_one, 1, flip=1)
    returned = lax.all_to_all(
        answers.reshape(replicas, capacity * cands, head_dim), "replica", split_axis=0, concat_axis=0, tiled=True
    )
    gated = pl.pallas_call(
        gate_kernel,
        in_specs=[ANY, HBM],
        out_specs=HBM,
        out_shape=jax.ShapeDtypeStruct((rows, head_dim), bf16),
        scratch_shapes=[
            pltpu.VMEM((slot_rows, head_dim), bf16),
            pltpu.VMEM((rows, 3 * head_dim), f32),
            pltpu.VMEM((rows, head_dim), bf16),
            pltpu.SemaphoreType.DMA((2,)),
        ],
        compiler_params=tight,
        cost_estimate=pl.CostEstimate(flops=1 << 30, bytes_accessed=64 << 20, transcendentals=1 << 10),
        name="gate",
    )(returned.reshape(slot_rows, head_dim), mine)
    share = rows // groups
    heads = lax.all_to_all(
        gated.reshape(groups, share, head_dim), "tensor", split_axis=0, concat_axis=0, tiled=True
    )
    return pl.pallas_call(
        output_kernel,
        in_specs=[SMEM, SMEM, HBM] + [VMEM] * 6,
        out_specs=HBM,
        out_shape=jax.ShapeDtypeStruct((share, model_width), bf16),
        scratch_shapes=[
            pltpu.VMEM((share, model_width), bf16),
            pltpu.VMEM((share, model_width), bf16),
            pltpu.SemaphoreType.DMA((2,)),
        ],
        compiler_params=roomy,
        name="output",
    )(group_index, my_index, tokens, heads, w_own, nexts, lasts, others, other_two)


def solution(mesh):
    in_specs = (
        P("replica", None),
        P(None, "tensor", None),
        P("tensor", None, None),
        P("replica", None, "tensor", None),
        P("replica", None, "tensor", None),
        P(),
        P("replica"),
        P("replica"),
        P(),
    )
    out_specs = P(("replica", "tensor"), None)
    return jax.shard_map(
        on_device, mesh=mesh, in_specs=in_specs, out_specs=out_specs, check_vma=False
    )
```

```python
import functools

import jax
import jax.numpy as jnp
from jax import lax
from jax.experimental import pallas as pl
from jax.experimental.pallas import tpu as pltpu
from jax.sharding import PartitionSpec as P

epsilon = 1e-05
f32 = jnp.float32
bf16 = jnp.bfloat16


def layer_norm(values):
    average = jnp.mean(values, -1, keepdims=True)
    centred = values - average
    return centred * lax.rsqrt(jnp.mean(centred * centred, -1, keepdims=True) + epsilon)


def silu(values):
    half = values * 0.5
    return half + half * jnp.tanh(half)


def iota(shape, dimension):
    return lax.broadcasted_iota(jnp.int32, shape, dimension)


def to_column(row):
    n = row.shape[1]
    return jnp.sum(jnp.where(iota((n, n), 0) == iota((n, n), 1), row, 0.0), 1, keepdims=True)


def lookup(table_row, index_row):
    sessions, requests = table_row.shape[1], index_row.shape[1]
    named = iota((sessions, requests), 0) == index_row
    return jnp.sum(jnp.where(named, to_column(table_row.astype(f32)), 0.0), 0, keepdims=True)


def first_rows(slot_ref, session_ref, capacity, cands):
    owner = lookup(slot_ref[...], session_ref[...])
    requests = owner.shape[1]
    square = (requests, requests)
    earlier = (to_column(owner) == owner) & (iota(square, 0) < iota(square, 1))
    rank = jnp.sum(jnp.where(earlier, 1.0, 0.0), 0, keepdims=True)
    return (owner * capacity + rank) * cands


def send_kernel(
    capacity, cands, chunks, tokens_ref, w_ref, slot_ref, session_ref, sent_ref,
    held, weight, queries, placed, sems, w_sem, out_sems,
):
    rows = tokens_ref.shape[0]
    head_dim = weight.shape[1]
    slot_rows = sent_ref.shape[0]
    chunk = rows // chunks
    fetch_w = pltpu.make_async_copy(w_ref.at[:, pl.ds(2 * head_dim, head_dim)], weight, w_sem)
    fetches = [
        pltpu.make_async_copy(
            tokens_ref.at[pl.ds(n * chunk, chunk), :], held.at[pl.ds(n * chunk, chunk), :], sems.at[n]
        )
        for n in range(chunks)
    ]
    fetches[0].start()
    fetch_w.start()
    for fetch in fetches[1:]:
        fetch.start()
    stores = []
    first = first_rows(slot_ref, session_ref, capacity, cands)
    requests = first.shape[1]
    spread = iota((requests, rows), 1) // cands == iota((requests, rows), 0)
    place = jnp.sum(jnp.where(spread, to_column(first), 0.0), 0, keepdims=True).astype(jnp.int32)
    place = place + iota((1, rows), 1) % cands
    for n, fetch in enumerate(fetches):
        part = pl.ds(n * chunk, chunk)
        fetch.wait()
        normed = layer_norm(held[part, :].astype(f32)).astype(bf16)
        if n == 0:
            fetch_w.wait()
        queries[part, :] = silu(jnp.dot(normed, weight[...], preferred_element_type=f32)).astype(bf16)
    block = slot_rows // chunks
    for n in range(chunks):
        part = pl.ds(n * block, block)
        chosen = jnp.where(iota((block, rows), 0) + n * block == place, 1.0, 0.0).astype(bf16)
        placed[part, :] = jnp.dot(chosen, queries[...], preferred_element_type=f32).astype(bf16)
        stores.append(pltpu.make_async_copy(placed.at[part, :], sent_ref.at[part, :], out_sems.at[n]))
        stores[-1].start()
    for store in stores:
        store.wait()


def local_kernel(
    capacity, cands, tokens_ref, w_ref, slot_ref, session_ref, count_ref, length_ref, me_ref, mine_ref, info_ref, result, sem
):
    rows = tokens_ref.shape[0]
    head_dim = result.shape[1] // 3
    normed = layer_norm(tokens_ref[...].astype(f32)).astype(bf16)
    projected = silu(jnp.dot(normed, w_ref[...], preferred_element_type=f32)).astype(bf16).astype(f32)
    gate = projected[:, :head_dim]
    values = projected[:, head_dim : 2 * head_dim]
    queries = projected[:, 2 * head_dim : 3 * head_dim]
    keys = projected[:, 3 * head_dim :]
    lengths = lookup(length_ref[...], session_ref[...])
    requests = lengths.shape[1]
    spread = iota((rows, requests), 0) // cands == iota((rows, requests), 1)

    def per_row(row):
        return jnp.sum(jnp.where(spread, row, 0.0), 1, keepdims=True)

    within = (iota((rows, 1), 0) % cands).astype(f32)
    scores = jnp.sum(queries * keys, -1, keepdims=True) * head_dim ** (-0.5)
    result[:, :head_dim] = silu(scores) * values / (per_row(lengths) + 1.0)
    alive = within < per_row(count_ref[...].astype(f32))
    result[:, head_dim : 2 * head_dim] = jnp.where(alive, gate, 0.0)
    place = per_row(first_rows(slot_ref, session_ref, capacity, cands)) + within
    result[:, 2 * head_dim :] = jnp.broadcast_to(place, (rows, head_dim))
    store = pltpu.make_async_copy(result, mine_ref, sem)
    store.start()
    own = slot_ref[...] == me_ref[0]
    held = jnp.sum(jnp.where(own, length_ref[...].astype(f32), 0.0), 1, keepdims=True)
    info_ref[...] = jnp.broadcast_to(held, info_ref.shape)
    store.wait()


def history_kernel(block, info_ref, query_ref, keys_ref, values_ref, out_ref, result, sems):
    history, head_dim = keys_ref.shape
    half_scale = 0.5 * head_dim ** (-0.5)
    length = info_ref[:1, :1]
    divisor = length + 1.0
    seen = iota((history, 1), 0).astype(f32) < length
    seen_values = jnp.where(seen, values_ref[...], jnp.zeros((), bf16))
    stores = []
    for n, start in enumerate(range(0, query_ref.shape[0], block)):
        part = pl.ds(start, block)
        half = (
            lax.dot_general(
                query_ref[part, :], keys_ref[...], (((1,), (1,)), ((), ())), preferred_element_type=f32
            )
            * half_scale
        )
        weights = (half + half * jnp.tanh(half)).astype(bf16)
        summed = jnp.dot(weights, seen_values, preferred_element_type=f32)
        result[part, :] = (summed / divisor).astype(bf16)
        stores.append(pltpu.make_async_copy(result.at[part, :], out_ref.at[part, :], sems.at[n]))
        stores[-1].start()
    for store in stores:
        store.wait()


def gate_kernel(returned_ref, mine_ref, out_ref, returned, mine, result, sems):
    fetches = [
        pltpu.make_async_copy(mine_ref, mine, sems.at[0]),
        pltpu.make_async_copy(returned_ref, returned, sems.at[1]),
    ]
    for fetch in fetches:
        fetch.start()
    rows, head_dim = result.shape
    slot_rows = returned.shape[0]
    fetches[0].wait()
    place = mine[:, 2 * head_dim : 2 * head_dim + 1].astype(jnp.int32)
    back = jnp.where(iota((rows, slot_rows), 1) == place, 1.0, 0.0).astype(bf16)
    fetches[1].wait()
    part = jnp.dot(back, returned[...], preferred_element_type=f32)
    result[...] = (layer_norm(part + mine[:, :head_dim]) * mine[:, head_dim : 2 * head_dim]).astype(bf16)
    store = pltpu.make_async_copy(result, out_ref, sems.at[0])
    store.start()
    store.wait()


def output_kernel(
    group_ref, me_ref, tokens_ref, gated_ref, own_ref, next_ref, last_ref, other_ref, two_ref,
    out_ref, tokens, result, sems,
):
    groups, share, head_dim = gated_ref.shape
    group = group_ref[0]
    mine = pl.ds(pl.multiple_of(group * share, share), share)
    fetch_tokens = pltpu.make_async_copy(tokens_ref.at[mine, :], tokens, sems.at[0])
    fetch_tokens.start()
    sign = jnp.where(me_ref[0] % 2 == 0, -1, 1)
    total = jnp.zeros(result.shape, f32)
    for heads, weight in (
        ((1, 3), next_ref[...]),
        ((2, 4), last_ref[...]),
        ((-1, -3), other_ref[...]),
        ((0, -2), jnp.concatenate([own_ref[...], two_ref[...]], axis=0)),
    ):
        rows = jnp.concatenate([gated_ref[lax.rem(group + sign * head + groups, groups)] for head in heads], axis=1)
        total = total + jnp.dot(rows, weight, preferred_element_type=f32)
    fetch_tokens.wait()
    result[...] = (tokens[...].astype(f32) + total).astype(bf16)
    store = pltpu.make_async_copy(result, out_ref, sems.at[1])
    store.start()
    store.wait()


ANY = pl.BlockSpec(memory_space=pl.ANY)
HBM = pl.BlockSpec(memory_space=pltpu.HBM)
VMEM = pl.BlockSpec(memory_space=pltpu.VMEM)
SMEM = pl.BlockSpec(memory_space=pltpu.SMEM)
params = pltpu.CompilerParams(vmem_limit_bytes=63 * 1024 * 1024)
tight = pltpu.CompilerParams(vmem_limit_bytes=54528 * 1024)
roomy = pltpu.CompilerParams(vmem_limit_bytes=24 * 1024 * 1024)


def after(value, other):
    return lax.optimization_barrier((value, other))[0]


def on_device(
    tokens,
    w_in,
    w_out,
    cache_keys,
    cache_values,
    session_slot,
    request_session,
    cand_count,
    hist_len,
):
    replicas = lax.axis_size("replica")
    groups = lax.axis_size("tensor")
    my_index = lax.axis_index("replica").astype(jnp.int32).reshape(1)
    group_index = lax.axis_index("tensor").astype(jnp.int32).reshape(1)
    rows, model_width = tokens.shape
    head_dim = w_in.shape[2] // 4
    requests = request_session.shape[0]
    cands = rows // requests
    history = cache_keys.shape[1]
    capacity = max(2, (2 * requests + replicas - 1) // replicas)
    slot_rows = replicas * capacity * cands
    w_flat = w_in.reshape(model_width, 4 * head_dim)
    slots = session_slot.reshape(1, -1)
    lengths = hist_len.reshape(1, -1)
    named = request_session.reshape(1, -1)
    counts = cand_count.reshape(1, -1)
    chunks = 4

    sent = pl.pallas_call(
        functools.partial(send_kernel, capacity, cands, chunks),
        in_specs=[HBM, HBM, VMEM, VMEM],
        out_specs=HBM,
        out_shape=jax.ShapeDtypeStruct((slot_rows, head_dim), bf16),
        scratch_shapes=[
            pltpu.VMEM((rows, model_width), bf16),
            pltpu.VMEM((model_width, head_dim), bf16),
            pltpu.VMEM((rows, head_dim), bf16),
            pltpu.VMEM((slot_rows, head_dim), bf16),
            pltpu.SemaphoreType.DMA((chunks,)),
            pltpu.SemaphoreType.DMA,
            pltpu.SemaphoreType.DMA((chunks,)),
        ],
        compiler_params=params,
        name="send",
    )(tokens, w_flat, slots, named)
    got = lax.all_to_all(
        sent.reshape(replicas, capacity * cands, head_dim), "replica", split_axis=0, concat_axis=0, tiled=True
    )
    def passed(piece, by, flip=0):
        pairs = []
        for r in range(replicas):
            for z in range(groups):
                pairs.append((r * groups + z, (r ^ flip) * groups + (z + (by if r % 2 == 0 else -by)) % groups))
        return lax.ppermute(piece, ("replica", "tensor"), pairs)

    def swapped(piece):
        return lax.ppermute(piece, "replica", [(r, r ^ 1) for r in range(replicas)])

    w_own = after(w_out.reshape(head_dim, model_width), sent)
    next_one = passed(w_own, 1)
    next_three = passed(w_own, 3)
    mine, info = pl.pallas_call(
        functools.partial(local_kernel, capacity, cands),
        in_specs=[VMEM] * 6 + [SMEM],
        out_specs=[HBM, VMEM],
        out_shape=[jax.ShapeDtypeStruct((rows, 3 * head_dim), f32), jax.ShapeDtypeStruct((8, 128), f32)],
        scratch_shapes=[pltpu.VMEM((rows, 3 * head_dim), f32), pltpu.SemaphoreType.DMA],
        compiler_params=roomy,
        cost_estimate=pl.CostEstimate(flops=1 << 30, bytes_accessed=16 << 20, transcendentals=1 << 18),
        name="local",
    )(tokens, w_flat, slots, after(named, sent), counts, lengths, my_index)
    block = min(256, slot_rows)
    answers = pl.pallas_call(
        functools.partial(history_kernel, block),
        in_specs=[VMEM] * 4,
        out_specs=HBM,
        out_shape=jax.ShapeDtypeStruct((slot_rows, head_dim), bf16),
        scratch_shapes=[
            pltpu.VMEM((slot_rows, head_dim), bf16),
            pltpu.SemaphoreType.DMA((slot_rows // block,)),
        ],
        compiler_params=roomy,
        cost_estimate=pl.CostEstimate(flops=1 << 30, bytes_accessed=64 << 20, transcendentals=slot_rows * history),
        name="history",
    )(
        info,
        got.reshape(slot_rows, head_dim),
        cache_keys.reshape(history, head_dim),
        cache_values.reshape(history, head_dim),
    )
    next_one, next_three = after((next_one, next_three), answers)
    nexts = jnp.concatenate([next_one, next_three], axis=0)
    lasts = passed(nexts, 1)
    others = swapped(nexts)
    other_two = passed(next_one, 1, flip=1)
    returned = lax.all_to_all(
        answers.reshape(replicas, capacity * cands, head_dim), "replica", split_axis=0, concat_axis=0, tiled=True
    )
    gated = pl.pallas_call(
        gate_kernel,
        in_specs=[ANY, HBM],
        out_specs=HBM,
        out_shape=jax.ShapeDtypeStruct((rows, head_dim), bf16),
        scratch_shapes=[
            pltpu.VMEM((slot_rows, head_dim), bf16),
            pltpu.VMEM((rows, 3 * head_dim), f32),
            pltpu.VMEM((rows, head_dim), bf16),
            pltpu.SemaphoreType.DMA((2,)),
        ],
        compiler_params=tight,
        cost_estimate=pl.CostEstimate(flops=1 << 30, bytes_accessed=64 << 20, transcendentals=1 << 10),
        name="gate",
    )(returned.reshape(slot_rows, head_dim), mine)
    share = rows // groups
    heads = lax.all_to_all(
        gated.reshape(groups, share, head_dim), "tensor", split_axis=0, concat_axis=0, tiled=True
    )
    return pl.pallas_call(
        output_kernel,
        in_specs=[SMEM, SMEM, HBM] + [VMEM] * 6,
        out_specs=HBM,
        out_shape=jax.ShapeDtypeStruct((share, model_width), bf16),
        scratch_shapes=[
            pltpu.VMEM((share, model_width), bf16),
            pltpu.VMEM((share, model_width), bf16),
            pltpu.SemaphoreType.DMA((2,)),
        ],
        compiler_params=roomy,
        name="output",
    )(group_index, my_index, tokens, heads, w_own, nexts, lasts, others, other_two)


def solution(mesh):
    in_specs = (
        P("replica", None),
        P(None, "tensor", None),
        P("tensor", None, None),
        P("replica", None, "tensor", None),
        P("replica", None, "tensor", None),
        P(),
        P("replica"),
        P("replica"),
        P(),
    )
    out_specs = P(("replica", "tensor"), None)
    return jax.shard_map(
        on_device, mesh=mesh, in_specs=in_specs, out_specs=out_specs, check_vma=False
    )
```

```python
import functools

import jax
import jax.numpy as jnp
from jax import lax
from jax.experimental import pallas as pl
from jax.experimental.pallas import tpu as pltpu
from jax.sharding import PartitionSpec as P

epsilon = 1e-05
f32 = jnp.float32
bf16 = jnp.bfloat16


def layer_norm(values):
    average = jnp.mean(values, -1, keepdims=True)
    centred = values - average
    return centred * lax.rsqrt(jnp.mean(centred * centred, -1, keepdims=True) + epsilon)


def silu(values):
    half = values * 0.5
    return half + half * jnp.tanh(half)


def iota(shape, dimension):
    return lax.broadcasted_iota(jnp.int32, shape, dimension)


def to_column(row):
    n = row.shape[1]
    return jnp.sum(jnp.where(iota((n, n), 0) == iota((n, n), 1), row, 0.0), 1, keepdims=True)


def lookup(table_row, index_row):
    sessions, requests = table_row.shape[1], index_row.shape[1]
    named = iota((sessions, requests), 0) == index_row
    return jnp.sum(jnp.where(named, to_column(table_row.astype(f32)), 0.0), 0, keepdims=True)


def first_rows(slot_ref, session_ref, capacity, cands):
    owner = lookup(slot_ref[...], session_ref[...])
    requests = owner.shape[1]
    square = (requests, requests)
    earlier = (to_column(owner) == owner) & (iota(square, 0) < iota(square, 1))
    rank = jnp.sum(jnp.where(earlier, 1.0, 0.0), 0, keepdims=True)
    return (owner * capacity + rank) * cands


def send_kernel(
    capacity, cands, chunks, tokens_ref, w_ref, slot_ref, session_ref, sent_ref,
    held, weight, queries, placed, chosen, sems, w_sem, out_sems,
):
    rows = tokens_ref.shape[0]
    head_dim = weight.shape[1]
    slot_rows = sent_ref.shape[0]
    chunk = rows // chunks
    fetch_w = pltpu.make_async_copy(w_ref.at[:, pl.ds(2 * head_dim, head_dim)], weight, w_sem)
    fetches = [
        pltpu.make_async_copy(
            tokens_ref.at[pl.ds(n * chunk, chunk), :], held.at[pl.ds(n * chunk, chunk), :], sems.at[n]
        )
        for n in range(chunks)
    ]
    fetches[0].start()
    fetch_w.start()
    for fetch in fetches[1:]:
        fetch.start()
    stores = []
    first = first_rows(slot_ref, session_ref, capacity, cands)
    requests = first.shape[1]
    spread = iota((requests, rows), 1) // cands == iota((requests, rows), 0)
    place = jnp.sum(jnp.where(spread, to_column(first), 0.0), 0, keepdims=True).astype(jnp.int32)
    place = place + iota((1, rows), 1) % cands
    chosen[...] = jnp.where(iota((slot_rows, rows), 0) == place, 1.0, 0.0).astype(bf16)
    for n, fetch in enumerate(fetches):
        part = pl.ds(n * chunk, chunk)
        fetch.wait()
        normed = layer_norm(held[part, :].astype(f32)).astype(bf16)
        if n == 0:
            fetch_w.wait()
        queries[part, :] = silu(jnp.dot(normed, weight[...], preferred_element_type=f32)).astype(bf16)
    block = slot_rows // chunks
    for n in range(chunks):
        part = pl.ds(n * block, block)
        placed[part, :] = jnp.dot(chosen[part, :], queries[...], preferred_element_type=f32).astype(bf16)
        stores.append(pltpu.make_async_copy(placed.at[part, :], sent_ref.at[part, :], out_sems.at[n]))
        stores[-1].start()
    for store in stores:
        store.wait()


def local_kernel(
    capacity, cands, chunks, tokens_ref, w_ref, slot_ref, session_ref, count_ref, length_ref, me_ref,
    mine_ref, info_ref, held, weight, result, sems, w_sem, out_sems,
):
    rows = tokens_ref.shape[0]
    head_dim = result.shape[1] // 3
    chunk = rows // chunks
    fetch_w = pltpu.make_async_copy(w_ref, weight, w_sem)
    fetches = []
    for n in range(chunks):
        part = pl.ds(n * chunk, chunk)
        fetches.append(pltpu.make_async_copy(tokens_ref.at[part, :], held.at[part, :], sems.at[n]))
    fetches[0].start()
    fetch_w.start()
    for fetch in fetches[1:]:
        fetch.start()
    own = slot_ref[...] == me_ref[0]
    length = jnp.sum(jnp.where(own, length_ref[...].astype(f32), 0.0), 1, keepdims=True)
    info_ref[...] = jnp.broadcast_to(length, info_ref.shape)
    lengths = lookup(length_ref[...], session_ref[...])
    counts = count_ref[...].astype(f32)
    first = first_rows(slot_ref, session_ref, capacity, cands)
    requests = lengths.shape[1]
    stores = []
    for n, fetch in enumerate(fetches):
        part = pl.ds(n * chunk, chunk)
        spread = (iota((chunk, requests), 0) + n * chunk) // cands == iota((chunk, requests), 1)

        def per_row(row):
            return jnp.sum(jnp.where(spread, row, 0.0), 1, keepdims=True)

        fetch.wait()
        normed = layer_norm(held[part, :].astype(f32)).astype(bf16)
        if n == 0:
            fetch_w.wait()
        projected = silu(jnp.dot(normed, weight[...], preferred_element_type=f32)).astype(bf16).astype(f32)
        gate = projected[:, :head_dim]
        values = projected[:, head_dim : 2 * head_dim]
        queries = projected[:, 2 * head_dim : 3 * head_dim]
        keys = projected[:, 3 * head_dim :]
        within = (iota((chunk, 1), 0) % cands).astype(f32)
        scores = jnp.sum(queries * keys, -1, keepdims=True) * head_dim ** (-0.5)
        result[part, :head_dim] = silu(scores) * values / (per_row(lengths) + 1.0)
        result[part, head_dim : 2 * head_dim] = jnp.where(within < per_row(counts), gate, 0.0)
        place = per_row(first) + within
        result[part, 2 * head_dim :] = jnp.broadcast_to(place, (chunk, head_dim))
        stores.append(pltpu.make_async_copy(result.at[part, :], mine_ref.at[part, :], out_sems.at[n]))
        stores[-1].start()
    for store in stores:
        store.wait()


def history_kernel(block, info_ref, query_ref, keys_ref, values_ref, out_ref, result, sems):
    history, head_dim = keys_ref.shape
    half_scale = 0.5 * head_dim ** (-0.5)
    length = info_ref[:1, :1]
    divisor = length + 1.0
    seen = iota((history, 1), 0).astype(f32) < length
    seen_values = jnp.where(seen, values_ref[...], jnp.zeros((), bf16))
    stores = []
    for n, start in enumerate(range(0, query_ref.shape[0], block)):
        part = pl.ds(start, block)
        half = (
            lax.dot_general(
                query_ref[part, :], keys_ref[...], (((1,), (1,)), ((), ())), preferred_element_type=f32
            )
            * half_scale
        )
        weights = (half + half * jnp.tanh(half)).astype(bf16)
        summed = jnp.dot(weights, seen_values, preferred_element_type=f32)
        result[part, :] = (summed / divisor).astype(bf16)
        stores.append(pltpu.make_async_copy(result.at[part, :], out_ref.at[part, :], sems.at[n]))
        stores[-1].start()
    for store in stores:
        store.wait()


def gate_kernel(returned_ref, mine_ref, out_ref, returned, mine, result, sems):
    fetches = [
        pltpu.make_async_copy(mine_ref, mine, sems.at[0]),
        pltpu.make_async_copy(returned_ref, returned, sems.at[1]),
    ]
    for fetch in fetches:
        fetch.start()
    rows, head_dim = result.shape
    slot_rows = returned.shape[0]
    fetches[0].wait()
    place = mine[:, 2 * head_dim : 2 * head_dim + 1].astype(jnp.int32)
    back = jnp.where(iota((rows, slot_rows), 1) == place, 1.0, 0.0).astype(bf16)
    fetches[1].wait()
    part = jnp.dot(back, returned[...], preferred_element_type=f32)
    result[...] = (layer_norm(part + mine[:, :head_dim]) * mine[:, head_dim : 2 * head_dim]).astype(bf16)
    store = pltpu.make_async_copy(result, out_ref, sems.at[0])
    store.start()
    store.wait()


def output_kernel(
    group_ref, me_ref, tokens_ref, gated_ref, own_ref, next_ref, last_ref, other_ref, two_ref,
    out_ref, tokens, result, sems,
):
    groups, share, head_dim = gated_ref.shape
    group = group_ref[0]
    mine = pl.ds(pl.multiple_of(group * share, share), share)
    fetch_tokens = pltpu.make_async_copy(tokens_ref.at[mine, :], tokens, sems.at[0])
    fetch_tokens.start()
    sign = jnp.where(me_ref[0] % 2 == 0, -1, 1)
    total = jnp.zeros(result.shape, f32)
    for heads, weight in (
        ((1, 3), next_ref[...]),
        ((2, 4), last_ref[...]),
        ((-1, -3), other_ref[...]),
        ((0, -2), jnp.concatenate([own_ref[...], two_ref[...]], axis=0)),
    ):
        rows = jnp.concatenate([gated_ref[lax.rem(group + sign * head + groups, groups)] for head in heads], axis=1)
        total = total + jnp.dot(rows, weight, preferred_element_type=f32)
    fetch_tokens.wait()
    result[...] = (tokens[...].astype(f32) + total).astype(bf16)
    store = pltpu.make_async_copy(result, out_ref, sems.at[1])
    store.start()
    store.wait()


ANY = pl.BlockSpec(memory_space=pl.ANY)
HBM = pl.BlockSpec(memory_space=pltpu.HBM)
VMEM = pl.BlockSpec(memory_space=pltpu.VMEM)
SMEM = pl.BlockSpec(memory_space=pltpu.SMEM)
params = pltpu.CompilerParams(vmem_limit_bytes=63 * 1024 * 1024)
tight = pltpu.CompilerParams(vmem_limit_bytes=54528 * 1024)
middle = pltpu.CompilerParams(vmem_limit_bytes=53760 * 1024)
roomy = pltpu.CompilerParams(vmem_limit_bytes=24 * 1024 * 1024)


def after(value, other):
    return lax.optimization_barrier((value, other))[0]


def on_device(
    tokens,
    w_in,
    w_out,
    cache_keys,
    cache_values,
    session_slot,
    request_session,
    cand_count,
    hist_len,
):
    replicas = lax.axis_size("replica")
    groups = lax.axis_size("tensor")
    my_index = lax.axis_index("replica").astype(jnp.int32).reshape(1)
    group_index = lax.axis_index("tensor").astype(jnp.int32).reshape(1)
    rows, model_width = tokens.shape
    head_dim = w_in.shape[2] // 4
    requests = request_session.shape[0]
    cands = rows // requests
    history = cache_keys.shape[1]
    capacity = max(2, (2 * requests + replicas - 1) // replicas)
    slot_rows = replicas * capacity * cands
    w_flat = w_in.reshape(model_width, 4 * head_dim)
    slots = session_slot.reshape(1, -1)
    lengths = hist_len.reshape(1, -1)
    named = request_session.reshape(1, -1)
    counts = cand_count.reshape(1, -1)
    chunks = 4

    sent = pl.pallas_call(
        functools.partial(send_kernel, capacity, cands, chunks),
        in_specs=[HBM, HBM, VMEM, VMEM],
        out_specs=HBM,
        out_shape=jax.ShapeDtypeStruct((slot_rows, head_dim), bf16),
        scratch_shapes=[
            pltpu.VMEM((rows, model_width), bf16),
            pltpu.VMEM((model_width, head_dim), bf16),
            pltpu.VMEM((rows, head_dim), bf16),
            pltpu.VMEM((slot_rows, head_dim), bf16),
            pltpu.VMEM((slot_rows, rows), bf16),
            pltpu.SemaphoreType.DMA((chunks,)),
            pltpu.SemaphoreType.DMA,
            pltpu.SemaphoreType.DMA((chunks,)),
        ],
        compiler_params=params,
        name="send",
    )(tokens, w_flat, slots, named)
    got = lax.all_to_all(
        sent.reshape(replicas, capacity * cands, head_dim), "replica", split_axis=0, concat_axis=0, tiled=True
    )
    def passed(piece, by, flip=0):
        pairs = []
        for r in range(replicas):
            for z in range(groups):
                pairs.append((r * groups + z, (r ^ flip) * groups + (z + (by if r % 2 == 0 else -by)) % groups))
        return lax.ppermute(piece, ("replica", "tensor"), pairs)

    def swapped(piece):
        return lax.ppermute(piece, "replica", [(r, r ^ 1) for r in range(replicas)])

    w_own = after(w_out.reshape(head_dim, model_width), sent)
    next_one = passed(w_own, 1)
    next_three = passed(w_own, 3)
    mine, info = pl.pallas_call(
        functools.partial(local_kernel, capacity, cands, chunks),
        in_specs=[HBM] * 2 + [VMEM] * 4 + [SMEM],
        out_specs=[HBM, VMEM],
        out_shape=[jax.ShapeDtypeStruct((rows, 3 * head_dim), f32), jax.ShapeDtypeStruct((8, 128), f32)],
        scratch_shapes=[
            pltpu.VMEM((rows, model_width), bf16),
            pltpu.VMEM((model_width, 4 * head_dim), bf16),
            pltpu.VMEM((rows, 3 * head_dim), f32),
            pltpu.SemaphoreType.DMA((chunks,)),
            pltpu.SemaphoreType.DMA,
            pltpu.SemaphoreType.DMA((chunks,)),
        ],
        compiler_params=middle,
        cost_estimate=pl.CostEstimate(flops=1 << 30, bytes_accessed=16 << 20, transcendentals=1 << 18),
        name="local",
    )(tokens, w_flat, slots, after(named, sent), counts, lengths, my_index)
    block = min(256, slot_rows)
    answers = pl.pallas_call(
        functools.partial(history_kernel, block),
        in_specs=[VMEM] * 4,
        out_specs=HBM,
        out_shape=jax.ShapeDtypeStruct((slot_rows, head_dim), bf16),
        scratch_shapes=[
            pltpu.VMEM((slot_rows, head_dim), bf16),
            pltpu.SemaphoreType.DMA((slot_rows // block,)),
        ],
        compiler_params=roomy,
        cost_estimate=pl.CostEstimate(flops=1 << 30, bytes_accessed=64 << 20, transcendentals=slot_rows * history),
        name="history",
    )(
        info,
        got.reshape(slot_rows, head_dim),
        cache_keys.reshape(history, head_dim),
        cache_values.reshape(history, head_dim),
    )
    next_one, next_three = after((next_one, next_three), answers)
    nexts = jnp.concatenate([next_one, next_three], axis=0)
    lasts = passed(nexts, 1)
    others = swapped(nexts)
    other_two = passed(next_one, 1, flip=1)
    returned = lax.all_to_all(
        answers.reshape(replicas, capacity * cands, head_dim), "replica", split_axis=0, concat_axis=0, tiled=True
    )
    gated = pl.pallas_call(
        gate_kernel,
        in_specs=[ANY, HBM],
        out_specs=HBM,
        out_shape=jax.ShapeDtypeStruct((rows, head_dim), bf16),
        scratch_shapes=[
            pltpu.VMEM((slot_rows, head_dim), bf16),
            pltpu.VMEM((rows, 3 * head_dim), f32),
            pltpu.VMEM((rows, head_dim), bf16),
            pltpu.SemaphoreType.DMA((2,)),
        ],
        compiler_params=tight,
        cost_estimate=pl.CostEstimate(flops=1 << 30, bytes_accessed=64 << 20, transcendentals=1 << 10),
        name="gate",
    )(returned.reshape(slot_rows, head_dim), mine)
    share = rows // groups
    heads = lax.all_to_all(
        gated.reshape(groups, share, head_dim), "tensor", split_axis=0, concat_axis=0, tiled=True
    )
    return pl.pallas_call(
        output_kernel,
        in_specs=[SMEM, SMEM, HBM] + [VMEM] * 6,
        out_specs=HBM,
        out_shape=jax.ShapeDtypeStruct((share, model_width), bf16),
        scratch_shapes=[
            pltpu.VMEM((share, model_width), bf16),
            pltpu.VMEM((share, model_width), bf16),
            pltpu.SemaphoreType.DMA((2,)),
        ],
        compiler_params=roomy,
        name="output",
    )(group_index, my_index, tokens, heads, w_own, nexts, lasts, others, other_two)


def solution(mesh):
    in_specs = (
        P("replica", None),
        P(None, "tensor", None),
        P("tensor", None, None),
        P("replica", None, "tensor", None),
        P("replica", None, "tensor", None),
        P(),
        P("replica"),
        P("replica"),
        P(),
    )
    out_specs = P(("replica", "tensor"), None)
    return jax.shard_map(
        on_device, mesh=mesh, in_specs=in_specs, out_specs=out_specs, check_vma=False
    )
```

```python
import functools

import jax
import jax.numpy as jnp
from jax import lax
from jax.experimental import pallas as pl
from jax.experimental.pallas import tpu as pltpu
from jax.sharding import PartitionSpec as P

epsilon = 1e-05
f32 = jnp.float32
bf16 = jnp.bfloat16


def layer_norm(values):
    average = jnp.mean(values, -1, keepdims=True)
    centred = values - average
    return centred * lax.rsqrt(jnp.mean(centred * centred, -1, keepdims=True) + epsilon)


def silu(values):
    half = values * 0.5
    return half + half * jnp.tanh(half)


def iota(shape, dimension):
    return lax.broadcasted_iota(jnp.int32, shape, dimension)


def to_column(row):
    n = row.shape[1]
    return jnp.sum(jnp.where(iota((n, n), 0) == iota((n, n), 1), row, 0.0), 1, keepdims=True)


def lookup(table_row, index_row):
    sessions, requests = table_row.shape[1], index_row.shape[1]
    named = iota((sessions, requests), 0) == index_row
    return jnp.sum(jnp.where(named, to_column(table_row.astype(f32)), 0.0), 0, keepdims=True)


def first_rows(slot_ref, session_ref, capacity, cands):
    owner = lookup(slot_ref[...], session_ref[...])
    requests = owner.shape[1]
    square = (requests, requests)
    earlier = (to_column(owner) == owner) & (iota(square, 0) < iota(square, 1))
    rank = jnp.sum(jnp.where(earlier, 1.0, 0.0), 0, keepdims=True)
    return (owner * capacity + rank) * cands


def send_kernel(
    capacity, cands, chunks, tokens_ref, w_ref, slot_ref, session_ref, sent_ref,
    held, weight, queries, placed, sems, w_sem, out_sems,
):
    rows = tokens_ref.shape[0]
    head_dim = weight.shape[1]
    slot_rows = sent_ref.shape[0]
    chunk = rows // chunks
    fetch_w = pltpu.make_async_copy(w_ref.at[:, pl.ds(2 * head_dim, head_dim)], weight, w_sem)
    fetches = [
        pltpu.make_async_copy(
            tokens_ref.at[pl.ds(n * chunk, chunk), :], held.at[pl.ds(n * chunk, chunk), :], sems.at[n]
        )
        for n in range(chunks)
    ]
    fetches[0].start()
    fetch_w.start()
    for fetch in fetches[1:]:
        fetch.start()
    stores = []
    first = first_rows(slot_ref, session_ref, capacity, cands)
    requests = first.shape[1]
    spread = iota((requests, rows), 1) // cands == iota((requests, rows), 0)
    place = jnp.sum(jnp.where(spread, to_column(first), 0.0), 0, keepdims=True).astype(jnp.int32)
    place = place + iota((1, rows), 1) % cands
    for n, fetch in enumerate(fetches):
        part = pl.ds(n * chunk, chunk)
        fetch.wait()
        normed = layer_norm(held[part, :].astype(f32)).astype(bf16)
        if n == 0:
            fetch_w.wait()
        queries[part, :] = silu(jnp.dot(normed, weight[...], preferred_element_type=f32)).astype(bf16)
    block = slot_rows // chunks
    for n in range(chunks):
        part = pl.ds(n * block, block)
        chosen = jnp.where(iota((block, rows), 0) + n * block == place, 1.0, 0.0).astype(bf16)
        placed[part, :] = jnp.dot(chosen, queries[...], preferred_element_type=f32).astype(bf16)
        stores.append(pltpu.make_async_copy(placed.at[part, :], sent_ref.at[part, :], out_sems.at[n]))
        stores[-1].start()
    for store in stores:
        store.wait()


def local_kernel(
    capacity, cands, tokens_ref, w_ref, slot_ref, session_ref, count_ref, length_ref, me_ref, mine_ref, info_ref, result, sem
):
    rows = tokens_ref.shape[0]
    head_dim = result.shape[1] // 3
    normed = layer_norm(tokens_ref[...].astype(f32)).astype(bf16)
    projected = silu(jnp.dot(normed, w_ref[...], preferred_element_type=f32)).astype(bf16).astype(f32)
    gate = projected[:, :head_dim]
    values = projected[:, head_dim : 2 * head_dim]
    queries = projected[:, 2 * head_dim : 3 * head_dim]
    keys = projected[:, 3 * head_dim :]
    lengths = lookup(length_ref[...], session_ref[...])
    requests = lengths.shape[1]
    spread = iota((rows, requests), 0) // cands == iota((rows, requests), 1)

    def per_row(row):
        return jnp.sum(jnp.where(spread, row, 0.0), 1, keepdims=True)

    within = (iota((rows, 1), 0) % cands).astype(f32)
    scores = jnp.sum(queries * keys, -1, keepdims=True) * head_dim ** (-0.5)
    result[:, :head_dim] = silu(scores) * values / (per_row(lengths) + 1.0)
    alive = within < per_row(count_ref[...].astype(f32))
    result[:, head_dim : 2 * head_dim] = jnp.where(alive, gate, 0.0)
    place = per_row(first_rows(slot_ref, session_ref, capacity, cands)) + within
    result[:, 2 * head_dim :] = jnp.broadcast_to(place, (rows, head_dim))
    store = pltpu.make_async_copy(result, mine_ref, sem)
    store.start()
    own = slot_ref[...] == me_ref[0]
    held = jnp.sum(jnp.where(own, length_ref[...].astype(f32), 0.0), 1, keepdims=True)
    info_ref[...] = jnp.broadcast_to(held, info_ref.shape)
    store.wait()


def history_kernel(block, info_ref, query_ref, keys_ref, values_ref, out_ref, result, sems):
    history, head_dim = keys_ref.shape
    half_scale = 0.5 * head_dim ** (-0.5)
    length = info_ref[:1, :1]
    divisor = length + 1.0
    seen = iota((history, 1), 0).astype(f32) < length
    seen_values = jnp.where(seen, values_ref[...], jnp.zeros((), bf16))
    stores = []
    for n, start in enumerate(range(0, query_ref.shape[0], block)):
        part = pl.ds(start, block)
        half = (
            lax.dot_general(
                query_ref[part, :], keys_ref[...], (((1,), (1,)), ((), ())), preferred_element_type=f32
            )
            * half_scale
        )
        weights = (half + half * jnp.tanh(half)).astype(bf16)
        summed = jnp.dot(weights, seen_values, preferred_element_type=f32)
        result[part, :] = (summed / divisor).astype(bf16)
        stores.append(pltpu.make_async_copy(result.at[part, :], out_ref.at[part, :], sems.at[n]))
        stores[-1].start()
    for store in stores:
        store.wait()


def gate_kernel(returned_ref, mine_ref, out_ref, returned, mine, result, sems):
    fetches = [
        pltpu.make_async_copy(mine_ref, mine, sems.at[0]),
        pltpu.make_async_copy(returned_ref, returned, sems.at[1]),
    ]
    for fetch in fetches:
        fetch.start()
    rows, head_dim = result.shape
    slot_rows = returned.shape[0]
    fetches[0].wait()
    place = mine[:, 2 * head_dim : 2 * head_dim + 1].astype(jnp.int32)
    back = jnp.where(iota((rows, slot_rows), 1) == place, 1.0, 0.0).astype(bf16)
    fetches[1].wait()
    part = jnp.dot(back, returned[...], preferred_element_type=f32)
    result[...] = (layer_norm(part + mine[:, :head_dim]) * mine[:, head_dim : 2 * head_dim]).astype(bf16)
    store = pltpu.make_async_copy(result, out_ref, sems.at[0])
    store.start()
    store.wait()


def output_kernel(
    group_ref, me_ref, tokens_ref, gated_ref, own_ref, next_ref, last_ref, other_ref, two_ref,
    out_ref, tokens, result, sems,
):
    groups, share, head_dim = gated_ref.shape
    group = group_ref[0]
    mine = pl.ds(pl.multiple_of(group * share, share), share)
    fetch_tokens = pltpu.make_async_copy(tokens_ref.at[mine, :], tokens, sems.at[0])
    fetch_tokens.start()
    sign = jnp.where(me_ref[0] % 2 == 0, -1, 1)
    total = jnp.zeros(result.shape, f32)
    for heads, weight in (
        ((1, 3), next_ref[...]),
        ((2, 4), last_ref[...]),
        ((-1, -3), other_ref[...]),
        ((0, -2), jnp.concatenate([own_ref[...], two_ref[...]], axis=0)),
    ):
        rows = jnp.concatenate([gated_ref[lax.rem(group + sign * head + groups, groups)] for head in heads], axis=1)
        total = total + jnp.dot(rows, weight, preferred_element_type=f32)
    fetch_tokens.wait()
    result[...] = (tokens[...].astype(f32) + total).astype(bf16)
    store = pltpu.make_async_copy(result, out_ref, sems.at[1])
    store.start()
    store.wait()


ANY = pl.BlockSpec(memory_space=pl.ANY)
HBM = pl.BlockSpec(memory_space=pltpu.HBM)
VMEM = pl.BlockSpec(memory_space=pltpu.VMEM)
SMEM = pl.BlockSpec(memory_space=pltpu.SMEM)
params = pltpu.CompilerParams(vmem_limit_bytes=63 * 1024 * 1024)
tight = pltpu.CompilerParams(vmem_limit_bytes=54528 * 1024)
roomy = pltpu.CompilerParams(vmem_limit_bytes=24 * 1024 * 1024)


def after(value, other):
    return lax.optimization_barrier((value, other))[0]


def on_device(
    tokens,
    w_in,
    w_out,
    cache_keys,
    cache_values,
    session_slot,
    request_session,
    cand_count,
    hist_len,
):
    replicas = lax.axis_size("replica")
    groups = lax.axis_size("tensor")
    my_index = lax.axis_index("replica").astype(jnp.int32).reshape(1)
    group_index = lax.axis_index("tensor").astype(jnp.int32).reshape(1)
    rows, model_width = tokens.shape
    head_dim = w_in.shape[2] // 4
    requests = request_session.shape[0]
    cands = rows // requests
    history = cache_keys.shape[1]
    capacity = max(2, (2 * requests + replicas - 1) // replicas)
    slot_rows = replicas * capacity * cands
    w_flat = w_in.reshape(model_width, 4 * head_dim)
    slots = session_slot.reshape(1, -1)
    lengths = hist_len.reshape(1, -1)
    named = request_session.reshape(1, -1)
    counts = cand_count.reshape(1, -1)
    chunks = 4

    sent = pl.pallas_call(
        functools.partial(send_kernel, capacity, cands, chunks),
        in_specs=[HBM, HBM, VMEM, VMEM],
        out_specs=HBM,
        out_shape=jax.ShapeDtypeStruct((slot_rows, head_dim), bf16),
        scratch_shapes=[
            pltpu.VMEM((rows, model_width), bf16),
            pltpu.VMEM((model_width, head_dim), bf16),
            pltpu.VMEM((rows, head_dim), bf16),
            pltpu.VMEM((slot_rows, head_dim), bf16),
            pltpu.SemaphoreType.DMA((chunks,)),
            pltpu.SemaphoreType.DMA,
            pltpu.SemaphoreType.DMA((chunks,)),
        ],
        compiler_params=params,
        name="send",
    )(tokens, w_flat, slots, named)
    got = lax.all_to_all(
        sent.reshape(replicas, capacity * cands, head_dim), "replica", split_axis=0, concat_axis=0, tiled=True
    )
    def passed(piece, by, flip=0):
        pairs = []
        for r in range(replicas):
            for z in range(groups):
                pairs.append((r * groups + z, (r ^ flip) * groups + (z + (by if r % 2 == 0 else -by)) % groups))
        return lax.ppermute(piece, ("replica", "tensor"), pairs)

    def swapped(piece):
        return lax.ppermute(piece, "replica", [(r, r ^ 1) for r in range(replicas)])

    mine, info = pl.pallas_call(
        functools.partial(local_kernel, capacity, cands),
        in_specs=[VMEM] * 6 + [SMEM],
        out_specs=[HBM, VMEM],
        out_shape=[jax.ShapeDtypeStruct((rows, 3 * head_dim), f32), jax.ShapeDtypeStruct((8, 128), f32)],
        scratch_shapes=[pltpu.VMEM((rows, 3 * head_dim), f32), pltpu.SemaphoreType.DMA],
        compiler_params=roomy,
        cost_estimate=pl.CostEstimate(flops=1 << 30, bytes_accessed=16 << 20, transcendentals=1 << 18),
        name="local",
    )(tokens, w_flat, slots, after(named, sent), counts, lengths, my_index)
    w_own = after(w_out.reshape(head_dim, model_width), mine)
    next_one = passed(w_own, 1)
    next_three = passed(w_own, 3)
    block = min(256, slot_rows)
    answers = pl.pallas_call(
        functools.partial(history_kernel, block),
        in_specs=[VMEM] * 4,
        out_specs=HBM,
        out_shape=jax.ShapeDtypeStruct((slot_rows, head_dim), bf16),
        scratch_shapes=[
            pltpu.VMEM((slot_rows, head_dim), bf16),
            pltpu.SemaphoreType.DMA((slot_rows // block,)),
        ],
        compiler_params=roomy,
        cost_estimate=pl.CostEstimate(flops=1 << 30, bytes_accessed=64 << 20, transcendentals=slot_rows * history),
        name="history",
    )(
        info,
        got.reshape(slot_rows, head_dim),
        cache_keys.reshape(history, head_dim),
        cache_values.reshape(history, head_dim),
    )
    next_one, next_three = after((next_one, next_three), answers)
    nexts = jnp.concatenate([next_one, next_three], axis=0)
    lasts = passed(nexts, 1)
    others = swapped(nexts)
    other_two = passed(next_one, 1, flip=1)
    returned = lax.all_to_all(
        answers.reshape(replicas, capacity * cands, head_dim), "replica", split_axis=0, concat_axis=0, tiled=True
    )
    gated = pl.pallas_call(
        gate_kernel,
        in_specs=[ANY, HBM],
        out_specs=HBM,
        out_shape=jax.ShapeDtypeStruct((rows, head_dim), bf16),
        scratch_shapes=[
            pltpu.VMEM((slot_rows, head_dim), bf16),
            pltpu.VMEM((rows, 3 * head_dim), f32),
            pltpu.VMEM((rows, head_dim), bf16),
            pltpu.SemaphoreType.DMA((2,)),
        ],
        compiler_params=tight,
        cost_estimate=pl.CostEstimate(flops=1 << 30, bytes_accessed=64 << 20, transcendentals=1 << 10),
        name="gate",
    )(returned.reshape(slot_rows, head_dim), mine)
    share = rows // groups
    heads = lax.all_to_all(
        gated.reshape(groups, share, head_dim), "tensor", split_axis=0, concat_axis=0, tiled=True
    )
    return pl.pallas_call(
        output_kernel,
        in_specs=[SMEM, SMEM, HBM] + [VMEM] * 6,
        out_specs=HBM,
        out_shape=jax.ShapeDtypeStruct((share, model_width), bf16),
        scratch_shapes=[
            pltpu.VMEM((share, model_width), bf16),
            pltpu.VMEM((share, model_width), bf16),
            pltpu.SemaphoreType.DMA((2,)),
        ],
        compiler_params=roomy,
        name="output",
    )(group_index, my_index, tokens, heads, w_own, nexts, lasts, others, other_two)


def solution(mesh):
    in_specs = (
        P("replica", None),
        P(None, "tensor", None),
        P("tensor", None, None),
        P("replica", None, "tensor", None),
        P("replica", None, "tensor", None),
        P(),
        P("replica"),
        P("replica"),
        P(),
    )
    out_specs = P(("replica", "tensor"), None)
    return jax.shard_map(
        on_device, mesh=mesh, in_specs=in_specs, out_specs=out_specs, check_vma=False
    )
```

```python
import functools

import jax
import jax.numpy as jnp
from jax import lax
from jax.experimental import pallas as pl
from jax.experimental.pallas import tpu as pltpu
from jax.sharding import PartitionSpec as P

epsilon = 1e-05
f32 = jnp.float32
bf16 = jnp.bfloat16


def layer_norm(values):
    average = jnp.mean(values, -1, keepdims=True)
    centred = values - average
    return centred * lax.rsqrt(jnp.mean(centred * centred, -1, keepdims=True) + epsilon)


def silu(values):
    half = values * 0.5
    return half + half * jnp.tanh(half)


def iota(shape, dimension):
    return lax.broadcasted_iota(jnp.int32, shape, dimension)


def to_column(row):
    n = row.shape[1]
    return jnp.sum(jnp.where(iota((n, n), 0) == iota((n, n), 1), row, 0.0), 1, keepdims=True)


def lookup(table_row, index_row):
    sessions, requests = table_row.shape[1], index_row.shape[1]
    named = iota((sessions, requests), 0) == index_row
    return jnp.sum(jnp.where(named, to_column(table_row.astype(f32)), 0.0), 0, keepdims=True)


def first_rows(slot_ref, session_ref, capacity, cands):
    owner = lookup(slot_ref[...], session_ref[...])
    requests = owner.shape[1]
    square = (requests, requests)
    earlier = (to_column(owner) == owner) & (iota(square, 0) < iota(square, 1))
    rank = jnp.sum(jnp.where(earlier, 1.0, 0.0), 0, keepdims=True)
    return (owner * capacity + rank) * cands


def send_kernel(
    capacity, cands, chunks, tokens_ref, w_ref, slot_ref, session_ref, sent_ref,
    held, weight, queries, placed, sems, w_sem, out_sems,
):
    rows = tokens_ref.shape[0]
    head_dim = weight.shape[1]
    slot_rows = sent_ref.shape[0]
    chunk = rows // chunks
    fetch_w = pltpu.make_async_copy(w_ref.at[:, pl.ds(2 * head_dim, head_dim)], weight, w_sem)
    fetches = [
        pltpu.make_async_copy(
            tokens_ref.at[pl.ds(n * chunk, chunk), :], held.at[pl.ds(n * chunk, chunk), :], sems.at[n]
        )
        for n in range(chunks)
    ]
    fetches[0].start()
    fetch_w.start()
    for fetch in fetches[1:]:
        fetch.start()
    stores = []
    first = first_rows(slot_ref, session_ref, capacity, cands)
    requests = first.shape[1]
    spread = iota((requests, rows), 1) // cands == iota((requests, rows), 0)
    place = jnp.sum(jnp.where(spread, to_column(first), 0.0), 0, keepdims=True).astype(jnp.int32)
    place = place + iota((1, rows), 1) % cands
    for n, fetch in enumerate(fetches):
        part = pl.ds(n * chunk, chunk)
        fetch.wait()
        normed = layer_norm(held[part, :].astype(f32)).astype(bf16)
        if n == 0:
            fetch_w.wait()
        queries[part, :] = silu(jnp.dot(normed, weight[...], preferred_element_type=f32)).astype(bf16)
    block = slot_rows // chunks
    for n in range(chunks):
        part = pl.ds(n * block, block)
        chosen = jnp.where(iota((block, rows), 0) + n * block == place, 1.0, 0.0).astype(bf16)
        placed[part, :] = jnp.dot(chosen, queries[...], preferred_element_type=f32).astype(bf16)
        stores.append(pltpu.make_async_copy(placed.at[part, :], sent_ref.at[part, :], out_sems.at[n]))
        stores[-1].start()
    for store in stores:
        store.wait()


def local_kernel(
    capacity, cands, tokens_ref, w_ref, slot_ref, session_ref, count_ref, length_ref, me_ref, mine_ref, info_ref, result, sem
):
    rows = tokens_ref.shape[0]
    head_dim = result.shape[1] // 3
    normed = layer_norm(tokens_ref[...].astype(f32)).astype(bf16)
    projected = silu(jnp.dot(normed, w_ref[...], preferred_element_type=f32)).astype(bf16).astype(f32)
    gate = projected[:, :head_dim]
    values = projected[:, head_dim : 2 * head_dim]
    queries = projected[:, 2 * head_dim : 3 * head_dim]
    keys = projected[:, 3 * head_dim :]
    lengths = lookup(length_ref[...], session_ref[...])
    requests = lengths.shape[1]
    spread = iota((rows, requests), 0) // cands == iota((rows, requests), 1)

    def per_row(row):
        return jnp.sum(jnp.where(spread, row, 0.0), 1, keepdims=True)

    within = (iota((rows, 1), 0) % cands).astype(f32)
    scores = jnp.sum(queries * keys, -1, keepdims=True) * head_dim ** (-0.5)
    result[:, :head_dim] = silu(scores) * values / (per_row(lengths) + 1.0)
    alive = within < per_row(count_ref[...].astype(f32))
    result[:, head_dim : 2 * head_dim] = jnp.where(alive, gate, 0.0)
    place = per_row(first_rows(slot_ref, session_ref, capacity, cands)) + within
    result[:, 2 * head_dim :] = jnp.broadcast_to(place, (rows, head_dim))
    store = pltpu.make_async_copy(result, mine_ref, sem)
    store.start()
    own = slot_ref[...] == me_ref[0]
    held = jnp.sum(jnp.where(own, length_ref[...].astype(f32), 0.0), 1, keepdims=True)
    info_ref[...] = jnp.broadcast_to(held, info_ref.shape)
    store.wait()


def history_kernel(block, info_ref, query_ref, keys_ref, values_ref, out_ref, result, sems):
    history, head_dim = keys_ref.shape
    half_scale = 0.5 * head_dim ** (-0.5)
    length = info_ref[:1, :1]
    divisor = length + 1.0
    seen = iota((history, 1), 0).astype(f32) < length
    seen_values = jnp.where(seen, values_ref[...], jnp.zeros((), bf16))
    stores = []
    for n, start in enumerate(range(0, query_ref.shape[0], block)):
        part = pl.ds(start, block)
        half = (
            lax.dot_general(
                query_ref[part, :], keys_ref[...], (((1,), (1,)), ((), ())), preferred_element_type=f32
            )
            * half_scale
        )
        weights = (half + half * jnp.tanh(half)).astype(bf16)
        summed = jnp.dot(weights, seen_values, preferred_element_type=f32)
        result[part, :] = (summed / divisor).astype(bf16)
        stores.append(pltpu.make_async_copy(result.at[part, :], out_ref.at[part, :], sems.at[n]))
        stores[-1].start()
    for store in stores:
        store.wait()


def gate_kernel(returned_ref, mine_ref, out_ref, returned, mine, result, sems):
    fetches = [
        pltpu.make_async_copy(mine_ref, mine, sems.at[0]),
        pltpu.make_async_copy(returned_ref, returned, sems.at[1]),
    ]
    for fetch in fetches:
        fetch.start()
    rows, head_dim = result.shape
    slot_rows = returned.shape[0]
    fetches[0].wait()
    place = mine[:, 2 * head_dim : 2 * head_dim + 1].astype(jnp.int32)
    back = jnp.where(iota((rows, slot_rows), 1) == place, 1.0, 0.0).astype(bf16)
    fetches[1].wait()
    part = jnp.dot(back, returned[...], preferred_element_type=f32)
    result[...] = (layer_norm(part + mine[:, :head_dim]) * mine[:, head_dim : 2 * head_dim]).astype(bf16)
    store = pltpu.make_async_copy(result, out_ref, sems.at[0])
    store.start()
    store.wait()


def output_kernel(
    group_ref, me_ref, tokens_ref, gated_ref, own_ref, next_ref, last_ref, other_ref, three_ref,
    out_ref, tokens, result, sems,
):
    groups, share, head_dim = gated_ref.shape
    group = group_ref[0]
    mine = pl.ds(pl.multiple_of(group * share, share), share)
    fetch_tokens = pltpu.make_async_copy(tokens_ref.at[mine, :], tokens, sems.at[0])
    fetch_tokens.start()
    sign = jnp.where(me_ref[0] % 2 == 0, -1, 1)
    total = jnp.zeros(result.shape, f32)
    for heads, weight in (
        ((1, 2), next_ref[...]),
        ((3, 4), last_ref[...]),
        ((-1, -2), other_ref[...]),
        ((0, -3), jnp.concatenate([own_ref[...], three_ref[...]], axis=0)),
    ):
        rows = jnp.concatenate([gated_ref[lax.rem(group + sign * head + groups, groups)] for head in heads], axis=1)
        total = total + jnp.dot(rows, weight, preferred_element_type=f32)
    fetch_tokens.wait()
    result[...] = (tokens[...].astype(f32) + total).astype(bf16)
    store = pltpu.make_async_copy(result, out_ref, sems.at[1])
    store.start()
    store.wait()


ANY = pl.BlockSpec(memory_space=pl.ANY)
HBM = pl.BlockSpec(memory_space=pltpu.HBM)
VMEM = pl.BlockSpec(memory_space=pltpu.VMEM)
SMEM = pl.BlockSpec(memory_space=pltpu.SMEM)
params = pltpu.CompilerParams(vmem_limit_bytes=63 * 1024 * 1024)
tight = pltpu.CompilerParams(vmem_limit_bytes=54528 * 1024)
roomy = pltpu.CompilerParams(vmem_limit_bytes=24 * 1024 * 1024)


def after(value, other):
    return lax.optimization_barrier((value, other))[0]


def on_device(
    tokens,
    w_in,
    w_out,
    cache_keys,
    cache_values,
    session_slot,
    request_session,
    cand_count,
    hist_len,
):
    replicas = lax.axis_size("replica")
    groups = lax.axis_size("tensor")
    my_index = lax.axis_index("replica").astype(jnp.int32).reshape(1)
    group_index = lax.axis_index("tensor").astype(jnp.int32).reshape(1)
    rows, model_width = tokens.shape
    head_dim = w_in.shape[2] // 4
    requests = request_session.shape[0]
    cands = rows // requests
    history = cache_keys.shape[1]
    capacity = max(2, (2 * requests + replicas - 1) // replicas)
    slot_rows = replicas * capacity * cands
    w_flat = w_in.reshape(model_width, 4 * head_dim)
    slots = session_slot.reshape(1, -1)
    lengths = hist_len.reshape(1, -1)
    named = request_session.reshape(1, -1)
    counts = cand_count.reshape(1, -1)
    chunks = 4

    sent = pl.pallas_call(
        functools.partial(send_kernel, capacity, cands, chunks),
        in_specs=[HBM, HBM, VMEM, VMEM],
        out_specs=HBM,
        out_shape=jax.ShapeDtypeStruct((slot_rows, head_dim), bf16),
        scratch_shapes=[
            pltpu.VMEM((rows, model_width), bf16),
            pltpu.VMEM((model_width, head_dim), bf16),
            pltpu.VMEM((rows, head_dim), bf16),
            pltpu.VMEM((slot_rows, head_dim), bf16),
            pltpu.SemaphoreType.DMA((chunks,)),
            pltpu.SemaphoreType.DMA,
            pltpu.SemaphoreType.DMA((chunks,)),
        ],
        compiler_params=params,
        name="send",
    )(tokens, w_flat, slots, named)
    got = lax.all_to_all(
        sent.reshape(replicas, capacity * cands, head_dim), "replica", split_axis=0, concat_axis=0, tiled=True
    )
    def passed(piece, by, flip=0):
        pairs = []
        for r in range(replicas):
            for z in range(groups):
                pairs.append((r * groups + z, (r ^ flip) * groups + (z + (by if r % 2 == 0 else -by)) % groups))
        return lax.ppermute(piece, ("replica", "tensor"), pairs)

    def swapped(piece):
        return lax.ppermute(piece, "replica", [(r, r ^ 1) for r in range(replicas)])

    mine, info = pl.pallas_call(
        functools.partial(local_kernel, capacity, cands),
        in_specs=[VMEM] * 6 + [SMEM],
        out_specs=[HBM, VMEM],
        out_shape=[jax.ShapeDtypeStruct((rows, 3 * head_dim), f32), jax.ShapeDtypeStruct((8, 128), f32)],
        scratch_shapes=[pltpu.VMEM((rows, 3 * head_dim), f32), pltpu.SemaphoreType.DMA],
        compiler_params=roomy,
        cost_estimate=pl.CostEstimate(flops=1 << 30, bytes_accessed=16 << 20, transcendentals=1 << 18),
        name="local",
    )(tokens, w_flat, slots, after(named, sent), counts, lengths, my_index)
    w_own = after(w_out.reshape(head_dim, model_width), mine)
    next_one = passed(w_own, 1)
    next_two = passed(w_own, 2)
    block = min(256, slot_rows)
    answers = pl.pallas_call(
        functools.partial(history_kernel, block),
        in_specs=[VMEM] * 4,
        out_specs=HBM,
        out_shape=jax.ShapeDtypeStruct((slot_rows, head_dim), bf16),
        scratch_shapes=[
            pltpu.VMEM((slot_rows, head_dim), bf16),
            pltpu.SemaphoreType.DMA((slot_rows // block,)),
        ],
        compiler_params=roomy,
        cost_estimate=pl.CostEstimate(flops=1 << 30, bytes_accessed=64 << 20, transcendentals=slot_rows * history),
        name="history",
    )(
        info,
        got.reshape(slot_rows, head_dim),
        cache_keys.reshape(history, head_dim),
        cache_values.reshape(history, head_dim),
    )
    next_one, next_two = after((next_one, next_two), answers)
    nexts = jnp.concatenate([next_one, next_two], axis=0)
    lasts = passed(nexts, 2)
    others = swapped(nexts)
    other_three = passed(next_two, 1, flip=1)
    returned = lax.all_to_all(
        answers.reshape(replicas, capacity * cands, head_dim), "replica", split_axis=0, concat_axis=0, tiled=True
    )
    gated = pl.pallas_call(
        gate_kernel,
        in_specs=[ANY, HBM],
        out_specs=HBM,
        out_shape=jax.ShapeDtypeStruct((rows, head_dim), bf16),
        scratch_shapes=[
            pltpu.VMEM((slot_rows, head_dim), bf16),
            pltpu.VMEM((rows, 3 * head_dim), f32),
            pltpu.VMEM((rows, head_dim), bf16),
            pltpu.SemaphoreType.DMA((2,)),
        ],
        compiler_params=tight,
        cost_estimate=pl.CostEstimate(flops=1 << 30, bytes_accessed=64 << 20, transcendentals=1 << 10),
        name="gate",
    )(returned.reshape(slot_rows, head_dim), mine)
    share = rows // groups
    heads = lax.all_to_all(
        gated.reshape(groups, share, head_dim), "tensor", split_axis=0, concat_axis=0, tiled=True
    )
    return pl.pallas_call(
        output_kernel,
        in_specs=[SMEM, SMEM, HBM] + [VMEM] * 6,
        out_specs=HBM,
        out_shape=jax.ShapeDtypeStruct((share, model_width), bf16),
        scratch_shapes=[
            pltpu.VMEM((share, model_width), bf16),
            pltpu.VMEM((share, model_width), bf16),
            pltpu.SemaphoreType.DMA((2,)),
        ],
        compiler_params=roomy,
        name="output",
    )(group_index, my_index, tokens, heads, w_own, nexts, lasts, others, other_three)


def solution(mesh):
    in_specs = (
        P("replica", None),
        P(None, "tensor", None),
        P("tensor", None, None),
        P("replica", None, "tensor", None),
        P("replica", None, "tensor", None),
        P(),
        P("replica"),
        P("replica"),
        P(),
    )
    out_specs = P(("replica", "tensor"), None)
    return jax.shard_map(
        on_device, mesh=mesh, in_specs=in_specs, out_specs=out_specs, check_vma=False
    )
```
